512 devices in a mesh: ctx: 128 (over z, y, core), head: 4 (over x).
Axes of the slice: x: 4, y: 8, z: 8, core: 2. Of those that a mesh axis runs over, the one named last changes fastest.
Arguments:
- features: bfloat16 [32768, 1024], P('ctx', 'head'), may hold values from -30 to 30
- w_qkv: bfloat16 [1024, 3, 1024], P(None, None, 'head'), may hold values from -1 to 1
- block_links: int32 [256, 9], P('ctx'), may hold values from -1 to 255, as said below
- d_out: bfloat16 [32768, 1024], P('ctx', 'head'), may hold values from -6 to 6
Outputs:
- attended: bfloat16 [32768, 1024], P('ctx', 'head')
- grad_features: bfloat16 [32768, 1024], P('ctx', 'head')
The draws below stay inside these ranges and needn't reach their ends.
Inputs may be any that keep to these rules, and one draw needn't show every extreme that they name: `block_links`: row q lists in order the key blocks q - 1 to q + 1; then p - 1 to p + 1, p being the block on the previous coil turn; then n - 1 to n + 1, n being the block on the next coil turn. q - p and n - q lie between 3 and 5, and a distance of 5 occurs in both directions in every draw. A coil neighbour may be absent; the entries of an absent neighbour and entries outside the sequence are -1. Live entries of a row are distinct.
All inputs are finite; a program needn't handle non-finite values.
Results may differ from the reference program's by a relative error of at most 0.025.
Values may be sent and summed in bfloat16 or wider, within the bound.
A program may use at most 64 MiB of HBM per device.

```python
import jax
import jax.numpy as jnp
from jax import lax

D = 1024
HEADS = 8
HD = 128
BLK = 128
BPD = 2
TURN = 4
JIT = 1
BAND = 1
WIN = 1
TOKENS = 32768
NBLK = 256
NB = 9
REACH = 6


def draw_features(key, part):
    key_base = jax.random.fold_in(jax.random.fold_in(key, 11), 0)
    drawn = jnp.clip(jax.random.normal(key_base, (NBLK, BLK, D), jnp.float32), -6.0, 6.0)
    return drawn.reshape(NBLK * BLK, D).astype(jnp.bfloat16)


def draw_w_qkv(key, part):
    key_base = jax.random.fold_in(jax.random.fold_in(key, 23), 0)
    fan_scale = D ** (-0.5)
    base = jnp.clip(jax.random.normal(key_base, (D, 3, D), jnp.float32), -6.0, 6.0)
    return (base * fan_scale).astype(jnp.bfloat16)


def draw_block_links(key, part):
    key_back, key_ahead, key_back_live, key_ahead_live = jax.random.split(jax.random.fold_in(key, 37), 4)
    rows_all = jnp.arange(NBLK, dtype=jnp.int32)
    back = jax.random.randint(key_back, (NBLK,), TURN - JIT, TURN + JIT + 1).astype(jnp.int32)
    ahead = jax.random.randint(key_ahead, (NBLK,), TURN - JIT, TURN + JIT + 1).astype(jnp.int32)
    back_live = jax.random.randint(key_back_live, (NBLK,), 0, 4) > 0
    ahead_live = jax.random.randint(key_ahead_live, (NBLK,), 0, 4) > 0
    ahead = ahead.at[BPD - 1].set(TURN + JIT)
    ahead_live = ahead_live.at[BPD - 1].set(True)
    back = back.at[NBLK - BPD].set(TURN + JIT)
    back_live = back_live.at[NBLK - BPD].set(True)
    band_steps = jnp.arange(-BAND, BAND + 1, dtype=jnp.int32)[None, :]
    window_steps = jnp.arange(-WIN, WIN + 1, dtype=jnp.int32)[None, :]
    band_links = rows_all[:, None] + band_steps
    prior_links = jnp.where(back_live[:, None], (rows_all - back)[:, None] + window_steps, -1)
    later_links = jnp.where(ahead_live[:, None], (rows_all + ahead)[:, None] + window_steps, -1)
    links_all = jnp.concatenate([band_links, prior_links, later_links], axis=1)
    links_all = jnp.where((links_all >= 0) & (links_all < NBLK), links_all, -1)
    return links_all.astype(jnp.int32)


def shard_levels(stream_key, extent, pieces, low, top_value):
    def one(position, blocks):
        steps = jax.random.uniform(jax.random.fold_in(jax.random.fold_in(stream_key, 6), position), (blocks,), jnp.float32, low / len(pieces), top_value / len(pieces))
        return jnp.repeat(jnp.exp(steps), extent[position] // blocks).reshape((-1,) + (1,) * (len(extent) - position - 1))

    level = one(*pieces[0])
    for cut in pieces[1:]:
        level = level * one(*cut)
    return level


def scatter_about(stream_key, extent, deviation, bound, cuts=(), kind=jnp.bfloat16):
    values = deviation * jax.random.normal(stream_key, extent, jnp.float32)
    if cuts:
        values = values * shard_levels(stream_key, extent, cuts, -0.22, 0.18)
    return jnp.clip(values, -bound, bound).astype(kind)


def setup_inputs(seed: int = 0) -> dict:
    arg_keys = jax.random.split(jax.random.key(seed), 5)
    return {
        "features": draw_features(jax.random.fold_in(arg_keys[4], 71), 0),
        "w_qkv": draw_w_qkv(jax.random.fold_in(arg_keys[4], 71), 0),
        "block_links": draw_block_links(jax.random.fold_in(arg_keys[4], 71), 0),
        "d_out": scatter_about(arg_keys[3], (TOKENS, D), 1.0, 6.0, ((0, 128), (1, 4))),
    }


def rounded(values):
    return lax.optimization_barrier(values.astype(jnp.bfloat16)).astype(jnp.float32)


def reference(features, w_qkv, block_links, d_out):
    model_width = features.shape[1]
    w_flat = w_qkv.reshape(model_width, 3 * model_width)
    projected = jnp.dot(features, w_flat, preferred_element_type=jnp.float32).astype(jnp.bfloat16)
    block_shape = (NBLK, BLK, HEADS, HD)
    queries = projected[:, :model_width].reshape(block_shape)
    keys = projected[:, model_width:2 * model_width].reshape(block_shape)
    values = projected[:, 2 * model_width:].reshape(block_shape)
    grads = d_out.reshape(block_shape)
    score_scale = HD ** -0.5
    window_len = BPD + 2 * REACH
    window_shape = (window_len, BLK, HEADS, HD)
    group_count = NBLK // BPD

    def visit_group(running, inputs):
        key_acc, value_acc = running
        query_group, grad_group, link_group, group_index = inputs
        window_base = group_index * BPD - REACH

        def visit(window_sums, inner):
            key_win, value_win = window_sums
            query_block, grad_block, link_row = inner
            live_slot = link_row >= 0
            slot_index = jnp.where(live_slot, link_row, 0).astype(jnp.int32)
            local_index = jnp.where(live_slot, link_row - window_base, 0).astype(jnp.int32)
            picked_lookup_rows = keys[slot_index].reshape(NB * BLK, HEADS, HD).astype(jnp.float32)
            picked_content_rows = values[slot_index].reshape(NB * BLK, HEADS, HD).astype(jnp.float32)
            query_f = query_block.astype(jnp.float32)
            grad_f = grad_block.astype(jnp.float32)
            scores = jnp.einsum("qhd,khd->hqk", query_f, picked_lookup_rows) * score_scale
            key_mask = jnp.repeat(live_slot, BLK)[None, None, :]
            largest = jnp.max(jnp.where(key_mask, scores, -1e30), axis=-1, keepdims=True)
            exp_terms = jnp.where(key_mask, jnp.exp(scores - largest), 0.0)
            normalized = exp_terms / jnp.sum(exp_terms, axis=-1, keepdims=True)
            softmax_share = rounded(normalized)
            attended = jnp.einsum("hqk,khd->qhd", softmax_share, picked_content_rows).astype(jnp.bfloat16)
            row_dot = jnp.sum(grad_f * attended.astype(jnp.float32), axis=-1)
            value_part = jnp.einsum("hqk,qhd->khd", softmax_share, grad_f)
            probability_gradient = jnp.einsum("qhd,khd->hqk", grad_f, picked_content_rows)
            score_derivative = rounded(normalized * (probability_gradient - row_dot.T[:, :, None]))
            query_grad = (jnp.einsum("hqk,khd->qhd", score_derivative, picked_lookup_rows) * score_scale).astype(jnp.bfloat16)
            key_part = jnp.einsum("hqk,qhd->khd", score_derivative, query_f) * score_scale
            live_gate = live_slot.astype(key_part.dtype)[:, None, None, None]
            key_part = key_part.reshape(NB, BLK, HEADS, HD) * live_gate
            value_part = value_part.reshape(NB, BLK, HEADS, HD) * live_gate
            key_win = key_win.at[local_index].add(key_part)
            value_win = value_win.at[local_index].add(value_part)
            return (key_win, value_win), (attended, query_grad)

        start_win = (jnp.zeros(window_shape, jnp.float32), jnp.zeros(window_shape, jnp.float32))
        (key_win, value_win), (attended, query_grad) = lax.scan(
            visit, start_win, (query_group, grad_group, link_group))
        acc_start = (group_index * BPD).astype(jnp.int32)
        zero_index = jnp.zeros((), jnp.int32)
        starts = (acc_start, zero_index, zero_index, zero_index)
        key_old = lax.dynamic_slice(key_acc, starts, window_shape)
        value_old = lax.dynamic_slice(value_acc, starts, window_shape)
        key_acc = lax.dynamic_update_slice(key_acc, key_old + rounded(key_win), starts)
        value_acc = lax.dynamic_update_slice(value_acc, value_old + rounded(value_win), starts)
        return (key_acc, value_acc), (attended, query_grad)

    padded_shape = (NBLK + 2 * REACH, BLK, HEADS, HD)
    start_sums = (jnp.zeros(padded_shape, jnp.float32), jnp.zeros(padded_shape, jnp.float32))
    group_shape = (group_count, BPD, BLK, HEADS, HD)
    (key_acc, value_acc), (attended, query_grad) = lax.scan(
        visit_group, start_sums,
        (queries.reshape(group_shape), grads.reshape(group_shape),
         block_links.reshape(group_count, BPD, NB), jnp.arange(group_count, dtype=jnp.int32)))
    key_acc = key_acc[REACH:REACH + NBLK]
    value_acc = value_acc[REACH:REACH + NBLK]
    total_rows = NBLK * BLK
    grad_projected = jnp.concatenate([
        query_grad.reshape(total_rows, model_width),
        key_acc.astype(jnp.bfloat16).reshape(total_rows, model_width),
        value_acc.astype(jnp.bfloat16).reshape(total_rows, model_width)], axis=1)
    grad_features = jnp.dot(grad_projected, w_flat.T, preferred_element_type=jnp.float32).astype(jnp.bfloat16)
    return attended.reshape(total_rows, model_width), grad_features
```

```python
import functools
import math

import jax
import jax.numpy as jnp
from jax import lax
from jax.experimental import pallas as pl
from jax.experimental.pallas import tpu as pltpu
from jax.sharding import PartitionSpec as P

MESH = pl.DeviceIdType.MESH
BLK = 128
HD = 128
SH = 256
SCALE = HD ** (-0.5)
C2 = SCALE * math.log2(math.e)
DEAD = -1e30
F32 = jnp.float32
BF16 = jnp.bfloat16
DO, K, V, Q = range(4)
PAD = 2
ROWS = 24
FAR = (-2, -1, 1, 2)
SOURCE = {0: (0, 1), 1: (1, 0), 2: (1, 1), 5: (2, 0), 6: (2, 1), 7: (3, 0)}


def dot(a, b):
    return jnp.dot(a, b, preferred_element_type=F32)


def dot_t(a, b):
    return lax.dot_general(a, b, (((1,), (1,)), ((), ())), preferred_element_type=F32)


def fold8(x, op):
    return op(x.reshape(x.shape[0] // 8, 8, x.shape[1]), axis=0)


def kernel(
    nctx,
    nhead,
    feat,
    w,
    links,
    dout,
    att,
    gout,
    F,
    W,
    ACC,
    WIN,
    OTH,
    BQ,
    S,
    DP,
    PB,
    DSB,
    KT,
    VT,
    MX,
    STO,
    STI,
    DKV,
    AST,
    GP,
    GST,
    RSO,
    RSI,
    OUT,
    loc,
    xs,
    xr,
    ws,
    wr,
    bs,
    br,
    ss,
    sr,
    as_,
    ar,
    gs,
    gr,
    rs,
    rr,
):
    g = lax.axis_index("ctx")
    hx = lax.axis_index("head")
    core = lax.rem(g, 2)
    oth = 1 - core
    chip = g // 2
    nchip = nctx // 2

    def at(distance, which):
        return (lax.rem(chip + distance + nchip, nchip) * 2 + which, hx)

    right = (g, lax.rem(hx + 1, nhead))
    left = (g, lax.rem(hx + nhead - 1, nhead))
    partner = at(0, oth)
    own_col = pl.ds(pl.multiple_of(core * HD, HD), HD)
    oth_col = pl.ds(pl.multiple_of(oth * HD, HD), HD)
    A, B = pl.ds(0, BLK), pl.ds(BLK, BLK)

    barrier = pltpu.get_barrier_semaphore()
    peers = [right, left, partner]
    peers += [at(d, k) for d in (1, -1) for k in (0, 1)]
    peers += [at(d, core) for d in (2, -2)]
    for peer in peers:
        pl.semaphore_signal(barrier, inc=1, device_id=peer, device_id_type=MESH)

    load_f = pltpu.make_async_copy(feat, F.at[0], loc.at[0])
    load_f.start()
    load_w = pltpu.make_async_copy(w, W, loc.at[1])
    load_w.start()
    load_d = pltpu.make_async_copy(dout.at[:, own_col], WIN.at[DO, 3 + core], loc.at[2])
    load_d.start()

    base = chip * 4 - 6 - PAD
    row = lax.broadcasted_iota(jnp.int32, (ROWS, BLK), 0)
    for r in range(2):
        live = None
        for j in range(9):
            entry = links[r, j]
            hit = row == jnp.where(entry >= 0, entry - base, -1)
            live = hit if live is None else live | hit
        BQ[core, :, r * BLK : (r + 1) * BLK] = jnp.where(live, 0.0, DEAD).astype(F32)

    started = []

    def send(src, dst, s_sem, r_sem, to):
        c = pltpu.make_async_remote_copy(
            src_ref=src,
            dst_ref=dst,
            send_sem=s_sem,
            recv_sem=r_sem,
            device_id=to,
            device_id_type=MESH,
        )
        c.start()
        started.append(c)

    def arrived(dst, s_sem, r_sem):
        pltpu.make_async_remote_copy(
            src_ref=dst,
            dst_ref=dst,
            send_sem=s_sem,
            recv_sem=r_sem,
            device_id=partner,
            device_id_type=MESH,
        ).wait_recv()

    def x_arrived(slot, half, n):
        arrived(F.at[slot, half], xs.at[n], xr.at[n])

    def win_arrived(kind, slot):
        arrived(WIN.at[kind, slot], ws.at[kind, 0], wr.at[kind, slot])

    def spread(kind, own, other):
        send(other, WIN.at[kind, 3 + core], ws.at[kind, 0], wr.at[kind, 3 + core], partner)
        for n, (d, slot) in enumerate(((1, 1 + core), (-1, 5 + core))):
            send(own, WIN.at[kind, slot], ws.at[kind, 1 + 2 * n], wr.at[kind, slot], at(d, core))
            send(other, WIN.at[kind, slot], ws.at[kind, 2 + 2 * n], wr.at[kind, slot], at(d, oth))

    def relay(kind):
        win_arrived(kind, 2)
        send(WIN.at[kind, 2], WIN.at[kind, 0], ws.at[kind, 5], wr.at[kind, 0], at(1, core))
        win_arrived(kind, 5)
        send(WIN.at[kind, 5], WIN.at[kind, 7], ws.at[kind, 6], wr.at[kind, 7], at(-1, core))

    pl.semaphore_wait(barrier, len(peers))

    send(feat.at[A], F.at[1, A], xs.at[0], xr.at[0], right)
    send(feat.at[B], F.at[2, B], xs.at[3], xr.at[3], left)
    send(feat.at[B], F.at[1, B], xs.at[1], xr.at[1], right)
    send(feat.at[A], F.at[2, A], xs.at[2], xr.at[2], left)
    send(BQ.at[core], BQ.at[core], bs.at[0], br.at[0], partner)
    spread(DO, dout.at[:, own_col], dout.at[:, oth_col])

    def w_rows(step):
        s = lax.rem(hx + step + nhead, nhead)
        return pl.ds(pl.multiple_of(s * SH, SH), SH)

    load_f.wait()
    load_w.wait()
    for i in range(3):
        ACC[i] = dot(F[0], W[i, w_rows(0), :])
    x_arrived(1, A, 0)
    send(F.at[1, A], F.at[3, A], xs.at[4], xr.at[4], right)
    x_arrived(2, B, 3)
    send(F.at[2, B], F.at[3, B], xs.at[5], xr.at[5], left)
    x_arrived(1, B, 1)
    for i in range(3):
        ACC[i] += dot(F[1], W[i, w_rows(-1), :])
    x_arrived(2, A, 2)
    for i in range(3):
        ACC[i] += dot(F[2], W[i, w_rows(1), :])
    relay(DO)
    x_arrived(3, A, 4)
    x_arrived(3, B, 5)
    for kind, i in ((K, 1), (V, 2), (Q, 0)):
        full = (ACC[i] + dot(F[3], W[i, w_rows(2), :])).astype(BF16)
        low, high = full[:, :HD], full[:, HD:]
        WIN[kind, 3 + core] = jnp.where(core == 0, low, high)
        OTH[kind] = jnp.where(core == 0, high, low)
        spread(kind, WIN.at[kind, 3 + core], OTH.at[kind])

    win_arrived(Q, 3 + oth)
    load_d.wait()
    win_arrived(DO, 3 + oth)
    arrived(BQ.at[oth], bs.at[0], br.at[0])
    MX[...] = jnp.full(MX.shape, -3e38, F32)

    def scores(s):
        for b in range(2):
            wb = 2 * s + b
            kb = WIN[K, s, b * BLK : (b + 1) * BLK, :]
            vb = WIN[V, s, b * BLK : (b + 1) * BLK, :]
            rows = slice(wb * BLK, (wb + 1) * BLK)
            for half in range(2):
                cols = slice(half * SH, (half + 1) * SH)
                x = dot_t(kb, WIN[Q, 3 + half]) * C2 + BQ[half, wb + PAD : wb + PAD + 1, :]
                S[rows, cols] = x
                MX[:, cols] = jnp.maximum(MX[:, cols], fold8(x, jnp.max))
                DP[rows, cols] = dot_t(vb, WIN[DO, 3 + half])
        KT[:, s * SH : (s + 1) * SH] = WIN[K, s].T
        VT[:, s * SH : (s + 1) * SH] = WIN[V, s].T

    win_arrived(K, 3 + oth)
    win_arrived(V, 3 + oth)
    scores(3)
    scores(4)
    relay(K)
    relay(V)
    scores(2)
    scores(5)
    relay(Q)
    for s in (1, 6, 0, 7):
        win_arrived(K, s)
        win_arrived(V, s)
        scores(s)

    m = jnp.max(MX[...], axis=0, keepdims=True)
    step = 32

    def totals(n, carry):
        l, rd = carry
        rows = pl.ds(pl.multiple_of(n * step, step), step)
        e = jnp.exp2(S[rows, :] - m)
        S[rows, :] = e
        return l + fold8(e, jnp.sum), rd + fold8(e * DP[rows, :], jnp.sum)

    zero = jnp.zeros((8, 2 * SH), F32)
    l, rd = lax.fori_loop(0, 8 * SH // step, totals, (zero, zero))
    il = 1.0 / jnp.sum(l, axis=0, keepdims=True)
    rd = jnp.sum(rd, axis=0, keepdims=True) * il
    for n, d in enumerate(FAR):
        STO[n, 0:1, :] = m
        STO[n, 1:2, :] = il
        STO[n, 2:3, :] = rd
        first = 6 + PAD + 4 * d
        for half in range(2):
            STO[n, 4:8, half * SH : (half + 1) * SH] = BQ[half, first : first + 4, :]
        send(STO.at[n], STI.at[3 - n], ss.at[n], sr.at[3 - n], at(d, core))

    def weights(n, carry):
        rows = pl.ds(pl.multiple_of(n * step, step), step)
        p = S[rows, :] * il
        PB[rows, :] = p.astype(BF16)
        DSB[rows, :] = (p * (DP[rows, :] - rd)).astype(BF16)
        return carry

    lax.fori_loop(0, 8 * SH // step, weights, 0)
    out = dot(VT[...], PB[...]).T.astype(BF16)
    AST[0] = out[:SH]
    AST[1] = out[SH:]
    send(AST.at[oth], att.at[:, own_col], as_.at[0], ar.at[0], partner)
    att_own = pltpu.make_async_copy(AST.at[core], att.at[:, own_col], loc.at[3])
    att_own.start()

    def hand_over(i, low, high):
        GP[i, :, own_col] = jnp.where(core == 0, low, high)
        GST[i] = jnp.where(core == 0, high, low)
        send(GST.at[i], GP.at[i, :, own_col], gs.at[i], gr.at[i], partner)

    dq = (dot(KT[...], DSB[...]) * SCALE).T.astype(BF16)
    hand_over(0, dq[:SH], dq[SH:])

    own = slice(3 * SH, 5 * SH)
    DKV[0] = dot(DSB[own, :], WIN[Q, 3:5].reshape(2 * SH, HD))
    DKV[1] = dot(PB[own, :], WIN[DO, 3:5].reshape(2 * SH, HD))
    seen = set()
    for s in (2, 5, 1, 6, 0, 7):
        n, half = SOURCE[s]
        if n not in seen:
            seen.add(n)
            arrived(STI.at[n], ss.at[n], sr.at[n])
        if s not in (2, 5):
            win_arrived(DO, s)
            win_arrived(Q, s)
        cols = slice(half * SH, (half + 1) * SH)
        sm, sil, srd = (STI[n, i : i + 1, cols] for i in range(3))
        qs, ds = WIN[Q, s], WIN[DO, s]
        for e in range(4):
            rows = slice((e % 2) * BLK, (e % 2 + 1) * BLK)
            x = dot_t(WIN[K, 3 + e // 2, rows, :], qs) * C2 + STI[n, 4 + e : 5 + e, cols]
            p = jnp.exp2(x - sm) * sil
            t = p * (dot_t(WIN[V, 3 + e // 2, rows, :], ds) - srd)
            rows = slice(e * BLK, (e + 1) * BLK)
            DKV[0, rows, :] += dot(t.astype(BF16), qs)
            DKV[1, rows, :] += dot(p.astype(BF16), ds)
    dk = (DKV[0] * SCALE).astype(BF16)
    hand_over(1, dk[:SH], dk[SH:])
    dv = DKV[1].astype(BF16)
    hand_over(2, dv[:SH], dv[SH:])

    for i in range(3):
        arrived(GP.at[i, :, oth_col], gs.at[i], gr.at[i])

    def partial(step):
        rows = w_rows(step)
        return sum(dot_t(GP[i], W[i, rows, :]) for i in range(3))

    def pass_on(n, to):
        send(RSO.at[n], RSI.at[n], rs.at[n], rr.at[n], to)

    def rs_arrived(n):
        arrived(RSI.at[n], rs.at[n], rr.at[n])
        return RSI[n].astype(F32)

    gx = partial(2)
    RSO[0] = gx[:BLK].astype(BF16)
    pass_on(0, right)
    RSO[1] = gx[BLK:].astype(BF16)
    pass_on(1, left)
    g_r = partial(1)
    RSO[2] = g_r[BLK:].astype(BF16)
    pass_on(2, right)
    g_l = partial(-1)
    RSO[3] = g_l[:BLK].astype(BF16)
    pass_on(3, left)
    RSO[4] = (g_r[:BLK] + rs_arrived(0)).astype(BF16)
    pass_on(4, right)
    RSO[5] = (g_l[BLK:] + rs_arrived(1)).astype(BF16)
    pass_on(5, left)
    g_o = partial(0)
    g_a = g_o[:BLK] + rs_arrived(3)
    g_b = g_o[BLK:] + rs_arrived(2)
    OUT[:BLK] = (g_a + rs_arrived(4)).astype(BF16)
    OUT[BLK:] = (g_b + rs_arrived(5)).astype(BF16)
    store = pltpu.make_async_copy(OUT, gout, loc.at[4])
    store.start()
    att_own.wait()
    arrived(att.at[:, oth_col], as_.at[0], ar.at[0])
    for c in started:
        c.wait_send()
    store.wait()


def solution(mesh):
    nctx, nhead = mesh.shape["ctx"], mesh.shape["head"]

    def body(features, w_qkv, block_links, d_out):
        w = jnp.transpose(w_qkv, (1, 0, 2))
        any_spec = pl.BlockSpec(memory_space=pl.ANY)
        dma = pltpu.SemaphoreType.DMA
        vmem = pltpu.VMEM
        return tuple(
            pl.pallas_call(
                functools.partial(kernel, nctx, nhead),
                out_shape=[
                    jax.ShapeDtypeStruct((SH, SH), BF16),
                    jax.ShapeDtypeStruct((SH, SH), BF16),
                ],
                in_specs=[
                    any_spec,
                    any_spec,
                    pl.BlockSpec(memory_space=pltpu.SMEM),
                    any_spec,
                ],
                out_specs=[any_spec, any_spec],
                scratch_shapes=[
                    vmem((4, SH, SH), BF16),
                    vmem((3, 1024, SH), BF16),
                    vmem((3, SH, SH), F32),
                    vmem((4, 8, SH, HD), BF16),
                    vmem((4, SH, HD), BF16),
                    vmem((2, ROWS, SH), F32),
                    vmem((8 * SH, 2 * SH), F32),
                    vmem((8 * SH, 2 * SH), F32),
                    vmem((8 * SH, 2 * SH), BF16),
                    vmem((8 * SH, 2 * SH), BF16),
                    vmem((HD, 8 * SH), BF16),
                    vmem((HD, 8 * SH), BF16),
                    vmem((8, 2 * SH), F32),
                    vmem((4, 8, 2 * SH), F32),
                    vmem((4, 8, 2 * SH), F32),
                    vmem((2, 2 * SH, HD), F32),
                    vmem((2, SH, HD), BF16),
                    vmem((3, SH, SH), BF16),
                    vmem((3, SH, HD), BF16),
                    vmem((6, BLK, SH), BF16),
                    vmem((6, BLK, SH), BF16),
                    vmem((SH, SH), BF16),
                    dma((5,)),
                    dma((6,)),
                    dma((6,)),
                    dma((4, 7)),
                    dma((4, 8)),
                    dma((1,)),
                    dma((1,)),
                    dma((4,)),
                    dma((4,)),
                    dma((1,)),
                    dma((1,)),
                    dma((3,)),
                    dma((3,)),
                    dma((6,)),
                    dma((6,)),
                ],
                compiler_params=pltpu.CompilerParams(
                    collective_id=0,
                    has_side_effects=True,
                    vmem_limit_bytes=48 * 1024 * 1024,
                ),
            )(features, w, block_links, d_out)
        )

    return jax.shard_map(
        body,
        mesh=mesh,
        in_specs=(P("ctx", "head"), P(None, None, "head"), P("ctx", None), P("ctx", "head")),
        out_specs=(P("ctx", "head"), P("ctx", "head")),
        check_vma=False,
    )
```

```python
import functools
import math

import jax
import jax.numpy as jnp
from jax import lax
from jax.experimental import pallas as pl
from jax.experimental.pallas import tpu as pltpu
from jax.sharding import PartitionSpec as P

MESH = pl.DeviceIdType.MESH
BLK = 128
HD = 128
SH = 256
SCALE = HD ** (-0.5)
C2 = SCALE * math.log2(math.e)
DEAD = -1e30
F32 = jnp.float32
BF16 = jnp.bfloat16
DO, K, V, Q = range(4)
PAD = 2
ROWS = 24
FAR = (-2, -1, 1, 2)
SOURCE = {0: (0, 1), 1: (1, 0), 2: (1, 1), 5: (2, 0), 6: (2, 1), 7: (3, 0)}


def dot(a, b):
    return jnp.dot(a, b, preferred_element_type=F32)


def dot_t(a, b):
    return lax.dot_general(a, b, (((1,), (1,)), ((), ())), preferred_element_type=F32)


def fold8(x, op):
    return op(x.reshape(x.shape[0] // 8, 8, x.shape[1]), axis=0)


def kernel(
    nctx,
    nhead,
    feat,
    w,
    links,
    dout,
    att,
    gout,
    F,
    W,
    ACC,
    WIN,
    OTH,
    BQ,
    S,
    DP,
    PB,
    DSB,
    KT,
    VT,
    MX,
    STO,
    STI,
    DKV,
    AST,
    GP,
    GST,
    RSO,
    RSI,
    OUT,
    FF,
    FO,
    LK,
    loc,
    xs,
    xr,
    fs,
    fr,
    ws,
    wr,
    bs,
    br,
    ss,
    sr,
    as_,
    ar,
    gs,
    gr,
    rs,
    rr,
):
    g = lax.axis_index("ctx")
    hx = lax.axis_index("head")
    core = lax.rem(g, 2)
    oth = 1 - core
    chip = g // 2
    nchip = nctx // 2
    has = {-1: chip > 0, -2: chip > 1, 1: chip < nchip - 1, 2: chip < nchip - 2}
    far_slot, far_oth = 7 * core, 7 * oth
    far_here = ((core == 0) & has[-2]) | ((core == 1) & has[2])
    far_there = ((core == 1) & has[-2]) | ((core == 0) & has[2])

    def at(distance, which):
        return (lax.rem(chip + distance + nchip, nchip) * 2 + which, hx)

    right = (g, lax.rem(hx + 1, nhead))
    left = (g, lax.rem(hx + nhead - 1, nhead))
    partner = at(0, oth)
    own_col = pl.ds(pl.multiple_of(core * HD, HD), HD)
    oth_col = pl.ds(pl.multiple_of(oth * HD, HD), HD)
    A, B = pl.ds(0, BLK), pl.ds(BLK, BLK)

    load_l = pltpu.make_async_copy(links, LK, loc.at[5])
    load_l.start()
    barrier = pltpu.get_barrier_semaphore()
    for peer in (right, left, partner):
        pl.semaphore_signal(barrier, inc=1, device_id=peer, device_id_type=MESH)
    count = 3
    for d in (1, -1, 2, -2):
        count += 2 * has[d].astype(jnp.int32)

        @pl.when(has[d])
        def _():
            for which in (0, 1):
                pl.semaphore_signal(barrier, inc=1, device_id=at(d, which), device_id_type=MESH)

    load_f = pltpu.make_async_copy(feat, F.at[0], loc.at[0])
    load_f.start()
    load_w = pltpu.make_async_copy(w, W, loc.at[1])
    load_w.start()
    load_d = pltpu.make_async_copy(dout.at[:, own_col], WIN.at[DO, 3 + core], loc.at[2])
    load_d.start()

    for d, n, slots in ((-2, 0, (0,)), (-1, 1, (1, 2)), (1, 2, (5, 6)), (2, 3, (7,))):

        @pl.when(jnp.logical_not(has[d]))
        def _():
            for slot in slots:
                for kind in range(4):
                    WIN[kind, slot] = jnp.zeros((SH, HD), BF16)
            STI[n, 0:4] = jnp.zeros((4, 2 * SH), F32)
            STI[n, 4:8] = jnp.full((4, 2 * SH), DEAD, F32)

    base = chip * 4 - 6 - PAD
    row = lax.broadcasted_iota(jnp.int32, (ROWS, BLK), 0)
    load_l.wait()
    for r in range(2):
        live = None
        for j in range(9):
            entry = LK[r, j]
            hit = row == jnp.where(entry >= 0, entry - base, -1)
            live = hit if live is None else live | hit
        BQ[core, :, r * BLK : (r + 1) * BLK] = jnp.where(live, 0.0, DEAD).astype(F32)

    started = []

    def send(src, dst, s_sem, r_sem, to, when=None):
        c = pltpu.make_async_remote_copy(
            src_ref=src,
            dst_ref=dst,
            send_sem=s_sem,
            recv_sem=r_sem,
            device_id=to,
            device_id_type=MESH,
        )
        if when is None:
            c.start()
        else:
            pl.when(when)(c.start)
        started.append((c, when))

    def arrived(dst, s_sem, r_sem, when=None):
        c = pltpu.make_async_remote_copy(
            src_ref=dst,
            dst_ref=dst,
            send_sem=s_sem,
            recv_sem=r_sem,
            device_id=partner,
            device_id_type=MESH,
        )
        if when is None:
            c.wait_recv()
        else:
            pl.when(when)(c.wait_recv)

    near = {0: has[-2], 1: has[-1], 2: has[-1], 5: has[1], 6: has[1], 7: has[2]}

    def win_arrived(kind, slot, when=None):
        if isinstance(slot, int):
            when = near[slot]
        arrived(WIN.at[kind, slot], ws.at[kind, 0], wr.at[kind, slot], when)

    def to_partner(kind, slot, src, n, when=None):
        send(src, WIN.at[kind, slot], ws.at[kind, n], wr.at[kind, slot], partner, when)

    def spread(kind, own, other):
        to_partner(kind, 3 + core, other, 0)
        for n, (d, slot) in enumerate(((1, 1 + core), (-1, 5 + core))):
            send(own, WIN.at[kind, slot], ws.at[kind, 1 + 2 * n], wr.at[kind, slot], at(d, core), has[d])
            send(other, WIN.at[kind, slot], ws.at[kind, 2 + 2 * n], wr.at[kind, slot], at(d, oth), has[d])

    def relay(kind):
        for n, (d, slot, to) in enumerate(((1, 2, 0), (-1, 5, 7))):
            win_arrived(kind, slot)
            both = has[1] & has[-1]
            send(WIN.at[kind, slot], WIN.at[kind, to], ws.at[kind, 5 + n], wr.at[kind, to], at(d, core), both)

    class Gather:
        def __init__(self, src, buf, s, r, when):
            self.src, self.buf, self.s, self.r, self.when = src, buf, s, r, when

        def begin(self):
            src, buf = self.src, self.buf
            for n, slot, half, to in ((0, 1, A, right), (3, 2, B, left), (1, 1, B, right), (2, 2, A, left)):
                send(src.at[half], buf.at[slot, half], self.s.at[n], self.r.at[n], to, self.when)

        def wait(self, slot, half, n):
            arrived(self.buf.at[slot, half], self.s.at[n], self.r.at[n], self.when)

        def middle(self):
            buf = self.buf
            self.wait(1, A, 0)
            send(buf.at[1, A], buf.at[3, A], self.s.at[4], self.r.at[4], right, self.when)
            self.wait(2, B, 3)
            send(buf.at[2, B], buf.at[3, B], self.s.at[5], self.r.at[5], left, self.when)
            self.wait(1, B, 1)
            self.wait(2, A, 2)

        def end(self):
            self.wait(3, A, 4)
            self.wait(3, B, 5)

    def w_rows(step):
        s = lax.rem(hx + step + nhead, nhead)
        return pl.ds(pl.multiple_of(s * SH, SH), SH)

    def project(buf, i):
        total = None
        for slot, step in ((0, 0), (1, -1), (2, 1)):
            part = dot(buf[slot], W[i, w_rows(step), :])
            total = part if total is None else total + part
        ACC[i] = total

    def projected(buf, i):
        full = (ACC[i] + dot(buf[3], W[i, w_rows(2), :])).astype(BF16)
        low, high = full[:, :HD], full[:, HD:]
        return jnp.where(core == 0, low, high), jnp.where(core == 0, high, low)

    pl.semaphore_wait(barrier, count)

    mine = Gather(feat, F, xs, xr, None)
    far = Gather(FF.at[0], FF, fs, fr, far_here)
    mine.begin()
    out_far = ((core == 1) & has[2]) | ((core == 0) & has[-2])
    far_to = (lax.rem(chip + jnp.where(core == 1, 2, -2) + nchip, nchip) * 2 + oth, hx)
    send(feat, FF.at[0], fs.at[6], fr.at[6], far_to, out_far)
    send(BQ.at[core], BQ.at[core], bs.at[0], br.at[0], partner)
    spread(DO, dout.at[:, own_col], dout.at[:, oth_col])

    load_f.wait()
    load_w.wait()
    mine.middle()
    arrived(FF.at[0], fs.at[6], fr.at[6], far_here)
    far.begin()
    for i in range(3):
        project(F, i)
    relay(DO)
    mine.end()
    for kind, i in ((K, 1), (V, 2), (Q, 0)):
        WIN[kind, 3 + core], OTH[kind] = projected(F, i)
        spread(kind, WIN.at[kind, 3 + core], OTH.at[kind])
    far.middle()

    @pl.when(far_here)
    def _():
        for i in range(3):
            project(FF, i)

    win_arrived(Q, 3 + oth)
    load_d.wait()
    win_arrived(DO, 3 + oth)
    arrived(BQ.at[oth], bs.at[0], br.at[0])
    MX[...] = jnp.full(MX.shape, -3e38, F32)

    def scores(s):
        for b in range(2):
            wb = 2 * s + b
            kb = WIN[K, s, b * BLK : (b + 1) * BLK, :]
            vb = WIN[V, s, b * BLK : (b + 1) * BLK, :]
            rows = slice(wb * BLK, (wb + 1) * BLK)
            for half in range(2):
                cols = slice(half * SH, (half + 1) * SH)
                x = dot_t(kb, WIN[Q, 3 + half]) * C2 + BQ[half, wb + PAD : wb + PAD + 1, :]
                S[rows, cols] = x
                MX[:, cols] = jnp.maximum(MX[:, cols], fold8(x, jnp.max))
                DP[rows, cols] = dot_t(vb, WIN[DO, 3 + half])
        KT[:, s * SH : (s + 1) * SH] = WIN[K, s].T
        VT[:, s * SH : (s + 1) * SH] = WIN[V, s].T

    win_arrived(K, 3 + oth)
    win_arrived(V, 3 + oth)
    scores(3)
    scores(4)
    far.end()
    for kind, i in ((K, 1), (V, 2), (Q, 0)):

        @pl.when(far_here)
        def _():
            WIN[kind, far_slot], FO[kind] = projected(FF, i)

        to_partner(kind, far_slot, FO.at[kind], 5, far_here)
    for s in (2, 5, 1, 6):
        win_arrived(K, s)
        win_arrived(V, s)
        scores(s)
    win_arrived(K, far_oth, far_there)
    win_arrived(V, far_oth, far_there)
    win_arrived(Q, far_oth, far_there)
    scores(0)
    scores(7)

    m = jnp.max(MX[...], axis=0, keepdims=True)
    step = 32

    def totals(n, carry):
        l, rd = carry
        rows = pl.ds(pl.multiple_of(n * step, step), step)
        e = jnp.exp2(S[rows, :] - m)
        S[rows, :] = e
        return l + fold8(e, jnp.sum), rd + fold8(e * DP[rows, :], jnp.sum)

    zero = jnp.zeros((8, 2 * SH), F32)
    l, rd = lax.fori_loop(0, 8 * SH // step, totals, (zero, zero))
    il = 1.0 / jnp.sum(l, axis=0, keepdims=True)
    rd = jnp.sum(rd, axis=0, keepdims=True) * il
    for n, d in enumerate(FAR):
        STO[n, 0:1, :] = m
        STO[n, 1:2, :] = il
        STO[n, 2:3, :] = rd
        first = 6 + PAD + 4 * d
        for half in range(2):
            STO[n, 4:8, half * SH : (half + 1) * SH] = BQ[half, first : first + 4, :]
        send(STO.at[n], STI.at[3 - n], ss.at[n], sr.at[3 - n], at(d, core), has[d])

    def weights(n, carry):
        rows = pl.ds(pl.multiple_of(n * step, step), step)
        p = S[rows, :] * il
        PB[rows, :] = p.astype(BF16)
        DSB[rows, :] = (p * (DP[rows, :] - rd)).astype(BF16)
        return carry

    lax.fori_loop(0, 8 * SH // step, weights, 0)
    out = dot(VT[...], PB[...]).T.astype(BF16)
    AST[0] = out[:SH]
    AST[1] = out[SH:]
    send(AST.at[oth], att.at[:, own_col], as_.at[0], ar.at[0], partner)
    att_own = pltpu.make_async_copy(AST.at[core], att.at[:, own_col], loc.at[3])
    att_own.start()

    def hand_over(i, low, high):
        GP[i, :, own_col] = jnp.where(core == 0, low, high)
        GST[i] = jnp.where(core == 0, high, low)
        send(GST.at[i], GP.at[i, :, own_col], gs.at[i], gr.at[i], partner)

    dq = (dot(KT[...], DSB[...]) * SCALE).T.astype(BF16)
    hand_over(0, dq[:SH], dq[SH:])

    own = slice(3 * SH, 5 * SH)
    DKV[0] = dot(DSB[own, :], WIN[Q, 3:5].reshape(2 * SH, HD))
    DKV[1] = dot(PB[own, :], WIN[DO, 3:5].reshape(2 * SH, HD))
    seen = set()
    for s in (2, 5, 1, 6, 0, 7):
        n, half = SOURCE[s]
        if n not in seen:
            seen.add(n)
            arrived(STI.at[n], ss.at[n], sr.at[n], has[FAR[n]])
        if s in (1, 6, 0, 7):
            win_arrived(DO, s)
        if s in (1, 2, 5, 6):
            win_arrived(Q, s)
        cols = slice(half * SH, (half + 1) * SH)
        sm, sil, srd = (STI[n, i : i + 1, cols] for i in range(3))
        qs, ds = WIN[Q, s], WIN[DO, s]
        for e in range(4):
            rows = slice((e % 2) * BLK, (e % 2 + 1) * BLK)
            x = dot_t(WIN[K, 3 + e // 2, rows, :], qs) * C2 + STI[n, 4 + e : 5 + e, cols]
            p = jnp.exp2(x - sm) * sil
            t = p * (dot_t(WIN[V, 3 + e // 2, rows, :], ds) - srd)
            rows = slice(e * BLK, (e + 1) * BLK)
            DKV[0, rows, :] += dot(t.astype(BF16), qs)
            DKV[1, rows, :] += dot(p.astype(BF16), ds)
    dk = (DKV[0] * SCALE).astype(BF16)
    hand_over(1, dk[:SH], dk[SH:])
    dv = DKV[1].astype(BF16)
    hand_over(2, dv[:SH], dv[SH:])

    for i in range(3):
        arrived(GP.at[i, :, oth_col], gs.at[i], gr.at[i])

    def partial(step):
        rows = w_rows(step)
        return sum(dot_t(GP[i], W[i, rows, :]) for i in range(3))

    def pass_on(n, to):
        send(RSO.at[n], RSI.at[n], rs.at[n], rr.at[n], to)

    def rs_arrived(n):
        arrived(RSI.at[n], rs.at[n], rr.at[n])
        return RSI[n].astype(F32)

    gx = partial(2)
    RSO[0] = gx[:BLK].astype(BF16)
    pass_on(0, right)
    RSO[1] = gx[BLK:].astype(BF16)
    pass_on(1, left)
    g_r = partial(1)
    RSO[2] = g_r[BLK:].astype(BF16)
    pass_on(2, right)
    g_l = partial(-1)
    RSO[3] = g_l[:BLK].astype(BF16)
    pass_on(3, left)
    RSO[4] = (g_r[:BLK] + rs_arrived(0)).astype(BF16)
    pass_on(4, right)
    RSO[5] = (g_l[BLK:] + rs_arrived(1)).astype(BF16)
    pass_on(5, left)
    g_o = partial(0)
    g_a = g_o[:BLK] + rs_arrived(3)
    g_b = g_o[BLK:] + rs_arrived(2)
    OUT[:BLK] = (g_a + rs_arrived(4)).astype(BF16)
    OUT[BLK:] = (g_b + rs_arrived(5)).astype(BF16)
    store = pltpu.make_async_copy(OUT, gout, loc.at[4])
    store.start()
    att_own.wait()
    arrived(att.at[:, oth_col], as_.at[0], ar.at[0])
    for c, when in started:
        if when is None:
            c.wait_send()
        else:
            pl.when(when)(c.wait_send)
    store.wait()


def solution(mesh):
    nctx, nhead = mesh.shape["ctx"], mesh.shape["head"]

    def body(features, w_qkv, block_links, d_out):
        w = jnp.transpose(w_qkv, (1, 0, 2))
        any_spec = pl.BlockSpec(memory_space=pl.ANY)
        hbm_spec = pl.BlockSpec(memory_space=pltpu.HBM)
        dma = pltpu.SemaphoreType.DMA
        vmem = pltpu.VMEM
        return tuple(
            pl.pallas_call(
                functools.partial(kernel, nctx, nhead),
                out_shape=[
                    jax.ShapeDtypeStruct((SH, SH), BF16),
                    jax.ShapeDtypeStruct((SH, SH), BF16),
                ],
                in_specs=[hbm_spec] * 4,
                out_specs=[any_spec, any_spec],
                scratch_shapes=[
                    vmem((4, SH, SH), BF16),
                    vmem((3, 1024, SH), BF16),
                    vmem((3, SH, SH), F32),
                    vmem((4, 8, SH, HD), BF16),
                    vmem((4, SH, HD), BF16),
                    vmem((2, ROWS, SH), F32),
                    vmem((8 * SH, 2 * SH), F32),
                    vmem((8 * SH, 2 * SH), F32),
                    vmem((8 * SH, 2 * SH), BF16),
                    vmem((8 * SH, 2 * SH), BF16),
                    vmem((HD, 8 * SH), BF16),
                    vmem((HD, 8 * SH), BF16),
                    vmem((8, 2 * SH), F32),
                    vmem((4, 8, 2 * SH), F32),
                    vmem((4, 8, 2 * SH), F32),
                    vmem((2, 2 * SH, HD), F32),
                    vmem((2, SH, HD), BF16),
                    vmem((3, SH, SH), BF16),
                    vmem((3, SH, HD), BF16),
                    vmem((6, BLK, SH), BF16),
                    vmem((6, BLK, SH), BF16),
                    vmem((SH, SH), BF16),
                    vmem((4, SH, SH), BF16),
                    vmem((4, SH, HD), BF16),
                    pltpu.SMEM((2, 9), jnp.int32),
                    dma((6,)),
                    dma((6,)),
                    dma((6,)),
                    dma((7,)),
                    dma((7,)),
                    dma((4, 7)),
                    dma((4, 8)),
                    dma((1,)),
                    dma((1,)),
                    dma((4,)),
                    dma((4,)),
                    dma((1,)),
                    dma((1,)),
                    dma((3,)),
                    dma((3,)),
                    dma((6,)),
                    dma((6,)),
                ],
                compiler_params=pltpu.CompilerParams(
                    collective_id=0,
                    has_side_effects=True,
                    vmem_limit_bytes=60 * 1024 * 1024,
                ),
            )(features, w, block_links, d_out)
        )

    return jax.shard_map(
        body,
        mesh=mesh,
        in_specs=(P("ctx", "head"), P(None, None, "head"), P("ctx", None), P("ctx", "head")),
        out_specs=(P("ctx", "head"), P("ctx", "head")),
        check_vma=False,
    )
```

```python
import functools
import math

import jax
import jax.numpy as jnp
from jax import lax
from jax.experimental import pallas as pl
from jax.experimental.pallas import tpu as pltpu
from jax.sharding import PartitionSpec as P

MESH = pl.DeviceIdType.MESH
BLK = 128
HD = 128
HALF = 64
SH = 256
SCALE = HD ** (-0.5)
C2 = SCALE * math.log2(math.e)
DEAD = -1e30
F32 = jnp.float32
BF16 = jnp.bfloat16
DO, K, V, Q = range(4)
PAD = 2
ROWS = 24
PAIRS = ((3, 4), (0, 7), (2, 5), (1, 6))
ORDER = (0, 2, 1, 3)
FAR = (-2, -1, 1, 2)
SOURCE = {0: (0, 1), 1: (1, 0), 2: (1, 1), 5: (2, 0), 6: (2, 1), 7: (3, 0)}


def dot(a, b):
    return jnp.dot(a, b, preferred_element_type=F32)


def dot_t(a, b):
    return lax.dot_general(a, b, (((1,), (1,)), ((), ())), preferred_element_type=F32)


def fold8(x, op):
    return op(x.reshape(x.shape[0] // 8, 8, x.shape[1]), axis=0)


def kernel(
    nctx,
    nhead,
    feat,
    w,
    links,
    dout,
    att,
    gout,
    F,
    W,
    ACC,
    WIN,
    OTH,
    BQ,
    S,
    DP,
    PB,
    DSB,
    PK,
    TK,
    KS,
    KDP,
    MS,
    KT,
    VT,
    STO,
    STI,
    AST,
    GP,
    GST,
    RSO,
    RSI,
    OUT,
    FF,
    FO,
    LK,
    loc,
    xs,
    xr,
    fs,
    fr,
    ws,
    wr,
    bs,
    br,
    ss,
    sr,
    as_,
    ar,
    gs,
    gr,
    rs,
    rr,
):
    g = lax.axis_index("ctx")
    hx = lax.axis_index("head")
    core = lax.rem(g, 2)
    oth = 1 - core
    chip = g // 2
    nchip = nctx // 2
    has = {-1: chip > 0, -2: chip > 1, 1: chip < nchip - 1, 2: chip < nchip - 2}
    far_slot, far_oth = 7 * core, 7 * oth
    far_here = ((core == 0) & has[-2]) | ((core == 1) & has[2])
    far_there = ((core == 1) & has[-2]) | ((core == 0) & has[2])

    def at(distance, which):
        return (lax.rem(chip + distance + nchip, nchip) * 2 + which, hx)

    right = (g, lax.rem(hx + 1, nhead))
    left = (g, lax.rem(hx + nhead - 1, nhead))
    partner = at(0, oth)
    own_col = pl.ds(pl.multiple_of(core * HD, HD), HD)
    oth_col = pl.ds(pl.multiple_of(oth * HD, HD), HD)
    A, B = pl.ds(0, BLK), pl.ds(BLK, BLK)

    load_l = pltpu.make_async_copy(links, LK, loc.at[5])
    load_l.start()
    barrier = pltpu.get_barrier_semaphore()
    for peer in (right, left, partner):
        pl.semaphore_signal(barrier, inc=1, device_id=peer, device_id_type=MESH)
    count = 3
    for d in (1, -1, 2, -2):
        count += 2 * has[d].astype(jnp.int32)

        @pl.when(has[d])
        def _():
            for which in (0, 1):
                pl.semaphore_signal(barrier, inc=1, device_id=at(d, which), device_id_type=MESH)

    load_f = pltpu.make_async_copy(feat, F.at[0], loc.at[0])
    load_f.start()
    load_w = pltpu.make_async_copy(w, W, loc.at[1])
    load_w.start()
    load_d = pltpu.make_async_copy(dout.at[:, own_col], WIN.at[DO, 3 + core], loc.at[2])
    load_d.start()

    for d, n, slots in ((-2, 0, (0,)), (-1, 1, (1, 2)), (1, 2, (5, 6)), (2, 3, (7,))):

        @pl.when(jnp.logical_not(has[d]))
        def _():
            for slot in slots:
                for kind in range(4):
                    WIN[kind, slot] = jnp.zeros((SH, HD), BF16)
            STI[n, 0:4] = jnp.zeros((4, 2 * SH), F32)
            STI[n, 4:8] = jnp.full((4, 2 * SH), DEAD, F32)

    base = chip * 4 - 6 - PAD
    row = lax.broadcasted_iota(jnp.int32, (ROWS, BLK), 0)
    load_l.wait()
    for r in range(2):
        live = None
        for j in range(9):
            entry = LK[r, j]
            hit = row == jnp.where(entry >= 0, entry - base, -1)
            live = hit if live is None else live | hit
        BQ[core, :, r * BLK : (r + 1) * BLK] = jnp.where(live, 0.0, DEAD).astype(F32)

    started = []

    def send(src, dst, s_sem, r_sem, to, when=None):
        c = pltpu.make_async_remote_copy(
            src_ref=src,
            dst_ref=dst,
            send_sem=s_sem,
            recv_sem=r_sem,
            device_id=to,
            device_id_type=MESH,
        )
        if when is None:
            c.start()
        else:
            pl.when(when)(c.start)
        started.append((c, when))

    def arrived(dst, s_sem, r_sem, when=None):
        c = pltpu.make_async_remote_copy(
            src_ref=dst,
            dst_ref=dst,
            send_sem=s_sem,
            recv_sem=r_sem,
            device_id=partner,
            device_id_type=MESH,
        )
        if when is None:
            c.wait_recv()
        else:
            pl.when(when)(c.wait_recv)

    near = {0: has[-2], 1: has[-1], 2: has[-1], 5: has[1], 6: has[1], 7: has[2]}

    def win_arrived(kind, slot, when=None):
        if isinstance(slot, int):
            when = near[slot]
        arrived(WIN.at[kind, slot], ws.at[kind, 0], wr.at[kind, slot], when)

    def to_partner(kind, slot, src, n, when=None):
        send(src, WIN.at[kind, slot], ws.at[kind, n], wr.at[kind, slot], partner, when)

    def spread(kind, own, other):
        to_partner(kind, 3 + core, other, 0)
        for n, (d, slot) in enumerate(((1, 1 + core), (-1, 5 + core))):
            send(own, WIN.at[kind, slot], ws.at[kind, 1 + 2 * n], wr.at[kind, slot], at(d, core), has[d])
            send(other, WIN.at[kind, slot], ws.at[kind, 2 + 2 * n], wr.at[kind, slot], at(d, oth), has[d])

    def relay(kind):
        for n, (d, slot, to) in enumerate(((1, 2, 0), (-1, 5, 7))):
            win_arrived(kind, slot)
            both = has[1] & has[-1]
            send(WIN.at[kind, slot], WIN.at[kind, to], ws.at[kind, 5 + n], wr.at[kind, to], at(d, core), both)

    class Gather:
        def __init__(self, src, buf, s, r, when):
            self.src, self.buf, self.s, self.r, self.when = src, buf, s, r, when

        def begin(self):
            src, buf = self.src, self.buf
            for n, slot, half, to in ((0, 1, A, right), (3, 2, B, left), (1, 1, B, right), (2, 2, A, left)):
                send(src.at[half], buf.at[slot, half], self.s.at[n], self.r.at[n], to, self.when)

        def wait(self, slot, half, n):
            arrived(self.buf.at[slot, half], self.s.at[n], self.r.at[n], self.when)

        def pass_right(self):
            buf = self.buf
            send(buf.at[1, A], buf.at[3, A], self.s.at[4], self.r.at[4], right, self.when)

        def rest(self):
            buf = self.buf
            self.wait(2, B, 3)
            send(buf.at[2, B], buf.at[3, B], self.s.at[5], self.r.at[5], left, self.when)
            self.wait(1, B, 1)
            self.wait(2, A, 2)

        def end(self):
            self.wait(3, A, 4)
            self.wait(3, B, 5)

    def w_rows(step):
        s = lax.rem(hx + step + nhead, nhead)
        return pl.ds(pl.multiple_of(s * SH, SH), SH)

    def project(buf, i):
        total = None
        for slot, step in ((0, 0), (1, -1), (2, 1)):
            part = dot(buf[slot], W[i, w_rows(step), :])
            total = part if total is None else total + part
        ACC[i] = total

    def projected(buf, i):
        full = (ACC[i] + dot(buf[3], W[i, w_rows(2), :])).astype(BF16)
        low, high = full[:, :HD], full[:, HD:]
        return jnp.where(core == 0, low, high), jnp.where(core == 0, high, low)

    pl.semaphore_wait(barrier, count)

    mine = Gather(feat, F, xs, xr, None)
    far = Gather(FF.at[0], FF, fs, fr, far_here)
    mine.begin()
    out_far = ((core == 1) & has[2]) | ((core == 0) & has[-2])
    far_to = (lax.rem(chip + jnp.where(core == 1, 2, -2) + nchip, nchip) * 2 + oth, hx)
    send(feat, FF.at[0], fs.at[6], fr.at[6], far_to, out_far)
    send(BQ.at[core], BQ.at[core], bs.at[0], br.at[0], partner)
    for tab in (PB, DSB):
        tab[:SH, SH:] = jnp.zeros((SH, SH), BF16)
        tab[7 * SH :, :SH] = jnp.zeros((SH, SH), BF16)
    for tab in (PK, TK):
        for pos, e in enumerate(ORDER):
            where = slice(7 * SH, 8 * SH) if e < 2 else slice(0, SH)
            tab[pos * BLK : (pos + 1) * BLK, where] = jnp.zeros((BLK, SH), BF16)
    load_f.wait()
    load_w.wait()
    mine.wait(1, A, 0)
    mine.pass_right()
    spread(DO, dout.at[:, own_col], dout.at[:, oth_col])
    mine.rest()
    for i in range(3):
        project(F, i)
    mine.end()
    arrived(FF.at[0], fs.at[6], fr.at[6], far_here)
    far.begin()
    for kind, i in ((K, 1), (V, 2), (Q, 0)):
        WIN[kind, 3 + core], OTH[kind] = projected(F, i)
        spread(kind, WIN.at[kind, 3 + core], OTH.at[kind])
    relay(DO)

    win_arrived(Q, 3 + oth)
    load_d.wait()
    win_arrived(DO, 3 + oth)
    arrived(BQ.at[oth], bs.at[0], br.at[0])

    def lanes(s):
        return {0: (0,), 7: (1,)}.get(s, (0, 1))

    def scores(pair):
        tops = [None, None]
        for s in pair:
            for half in lanes(s):
                cols = slice(half * SH, (half + 1) * SH)
                x = dot_t(WIN[K, s], WIN[Q, 3 + half]) * C2
                for b in range(2):
                    wb = 2 * s + b + PAD
                    y = x[b * BLK : (b + 1) * BLK] + BQ[half, wb : wb + 1, :]
                    S[s * SH + b * BLK : s * SH + (b + 1) * BLK, cols] = y
                    top = fold8(y, jnp.max)
                    tops[half] = top if tops[half] is None else jnp.maximum(tops[half], top)
                DP[s * SH : (s + 1) * SH, cols] = dot_t(WIN[V, s], WIN[DO, 3 + half])
        return jnp.max(jnp.concatenate(tops, axis=1), axis=0, keepdims=True)

    def query_side(n, pair, m_old, l8, r8):
        m_new = jnp.maximum(m_old, scores(pair))
        MS[n] = m_new
        shrink = jnp.exp2(m_old - m_new)
        l8, r8 = l8 * shrink, r8 * shrink
        for s in pair:
            halves = lanes(s)
            cols = slice(halves[0] * SH, (halves[-1] + 1) * SH)
            step = 64 // len(halves)
            top = m_new[:, cols]

            def piece(i, carry):
                l, r = carry
                rows = pl.ds(pl.multiple_of(s * SH + i * step, step), step)
                e = jnp.exp2(S[rows, cols] - top)
                S[rows, cols] = e
                return l + fold8(e, jnp.sum), r + fold8(e * DP[rows, cols], jnp.sum)

            zero = jnp.zeros((8, SH * len(halves)), F32)
            l, r = lax.fori_loop(0, SH // step, piece, (zero, zero))
            if len(halves) == 1:
                pads = [jnp.zeros((8, SH), F32)] * 2
                pads[halves[0]] = l
                l = jnp.concatenate(pads, axis=1)
                pads[halves[0]] = r
                r = jnp.concatenate(pads, axis=1)
            l8, r8 = l8 + l, r8 + r
        return m_new, l8, r8

    win_arrived(K, 3 + oth)
    win_arrived(V, 3 + oth)
    m = jnp.full((1, 2 * SH), -3e38, F32)
    l8 = jnp.zeros((8, 2 * SH), F32)
    r8 = l8
    m, l8, r8 = query_side(0, PAIRS[0], m, l8, r8)

    far.wait(1, A, 0)
    far.pass_right()
    far.rest()

    @pl.when(far_here)
    def _():
        for i in range(3):
            project(FF, i)

    far.end()
    for kind, i in ((K, 1), (V, 2), (Q, 0)):

        @pl.when(far_here)
        def _():
            WIN[kind, far_slot], FO[kind] = projected(FF, i)

        to_partner(kind, far_slot, FO.at[kind], 5, far_here)
    for kind in (K, V):
        win_arrived(kind, far_oth, far_there)
    for n, pair in enumerate(PAIRS):
        if n == 0:
            continue
        if n > 1:
            for s in pair:
                win_arrived(K, s)
                win_arrived(V, s)
        m, l8, r8 = query_side(n, pair, m, l8, r8)

    il = 1.0 / jnp.sum(l8, axis=0, keepdims=True)
    rd = jnp.sum(r8, axis=0, keepdims=True) * il
    for n, d in enumerate(FAR):
        STO[n, 0:1, :] = m
        STO[n, 1:2, :] = il
        STO[n, 2:3, :] = rd
        first = 6 + PAD + 4 * d
        for half in range(2):
            STO[n, 4:8, half * SH : (half + 1) * SH] = BQ[half, first : first + 4, :]
        send(STO.at[n], STI.at[3 - n], ss.at[n], sr.at[3 - n], at(d, core), has[d])

    for n, pair in enumerate(PAIRS):
        factor = jnp.exp2(MS[n] - m) * il
        for s in pair:
            halves = lanes(s)
            cols = slice(halves[0] * SH, (halves[-1] + 1) * SH)
            step = 64 // len(halves)
            f, r0 = factor[:, cols], rd[:, cols]

            def piece(i, carry):
                rows = pl.ds(pl.multiple_of(s * SH + i * step, step), step)
                p = S[rows, cols] * f
                PB[rows, cols] = p.astype(BF16)
                DSB[rows, cols] = (p * (DP[rows, cols] - r0)).astype(BF16)
                return carry

            lax.fori_loop(0, SH // step, piece, 0)
    for s in range(8):
        KT[:, s * SH : (s + 1) * SH] = WIN[K, s].T
        VT[:, s * SH : (s + 1) * SH] = WIN[V, s].T
    out = dot(VT[...], PB[...]).T.astype(BF16)
    AST[0] = out[:SH]
    AST[1] = out[SH:]
    send(AST.at[oth], att.at[:, own_col], as_.at[0], ar.at[0], partner)
    att_own = pltpu.make_async_copy(AST.at[core], att.at[:, own_col], loc.at[3])
    att_own.start()

    def hand_over(i, n, low, high):
        rows = pl.ds(n * BLK, BLK)
        GP[i, rows, own_col] = jnp.where(core == 0, low, high)
        GST[i, rows] = jnp.where(core == 0, high, low)
        send(GST.at[i, rows], GP.at[i, rows, own_col], gs.at[i, n], gr.at[i, n], partner)

    dq = (dot(KT[...], DSB[...]) * SCALE).T.astype(BF16)
    for n in range(2):
        rows = slice(n * BLK, (n + 1) * BLK)
        hand_over(0, n, dq[rows], dq[SH:][rows])

    for pos, e in enumerate(ORDER):
        rows, keys = slice(pos * BLK, (pos + 1) * BLK), slice((6 + e) * BLK, (7 + e) * BLK)
        PK[rows, 3 * SH : 5 * SH] = PB[keys, :]
        TK[rows, 3 * SH : 5 * SH] = DSB[keys, :]

    def spans(s):
        return {0: (0,), 7: (1,)}.get(s, (0, 1))

    win_arrived(Q, far_oth, far_there)
    for s in (0, 7, 2, 5, 1, 6):
        if s in (1, 6, 0, 7):
            win_arrived(DO, s)
        if s in (1, 2, 5, 6):
            win_arrived(Q, s)
        for c in spans(s):
            rows = slice(c * SH, (c + 1) * SH)
            KS[s, rows] = dot_t(WIN[K, 3 + c], WIN[Q, s]) * C2
            KDP[s, rows] = dot_t(WIN[V, 3 + c], WIN[DO, s])
    for n, d in enumerate(FAR):
        arrived(STI.at[n], ss.at[n], sr.at[n], has[d])
    wide = (8 * SH, HD)
    for part in range(2):
        for s in (2, 5, 1, 6, 0, 7):
            n, half = SOURCE[s]
            cols = slice(half * SH, (half + 1) * SH)
            sm, sil, srd = (STI[n, i : i + 1, cols] for i in range(3))
            for c in spans(s):
                e = 2 * c + part
                pos = 2 * part + c
                shift = STI[n, 4 + e : 5 + e, cols] - sm

                def piece(i, carry):
                    src = pl.ds(pl.multiple_of(e * BLK + i * 64, 64), 64)
                    dst = pl.ds(pl.multiple_of(pos * BLK + i * 64, 64), 64)
                    p = jnp.exp2(KS[s, src] + shift) * sil
                    PK[dst, s * SH : (s + 1) * SH] = p.astype(BF16)
                    TK[dst, s * SH : (s + 1) * SH] = (p * (KDP[s, src] - srd)).astype(BF16)
                    return carry

                lax.fori_loop(0, BLK // 64, piece, 0)
        rows = slice(part * SH, (part + 1) * SH)
        dk = (dot(TK[rows, :], WIN[Q].reshape(wide)) * SCALE).astype(BF16)
        hand_over(1, part, dk[:BLK], dk[BLK:])
        dv = dot(PK[rows, :], WIN[DO].reshape(wide)).astype(BF16)
        hand_over(2, part, dv[:BLK], dv[BLK:])

    def partial(part, step):
        rows = w_rows(step)
        mine = slice(part * BLK, (part + 1) * BLK)
        return sum(dot_t(GP[i, mine, :], W[i, rows, :]) for i in range(3))

    def pass_on(part, n, value, to):
        RSO[part, n] = value.astype(BF16)
        send(RSO.at[part, n], RSI.at[part, n], rs.at[part, n], rr.at[part, n], to)

    def rs_arrived(part, n):
        arrived(RSI.at[part, n], rs.at[part, n], rr.at[part, n])
        return RSI[part, n].astype(F32)

    kept = []
    for part in range(2):
        for i in range(3):
            rows = pl.ds(part * BLK, BLK)
            arrived(GP.at[i, rows, oth_col], gs.at[i, part], gr.at[i, part])
        gx = partial(part, 2)
        pass_on(part, 0, gx[:HALF], right)
        pass_on(part, 1, gx[HALF:], left)
        g_r = partial(part, 1)
        pass_on(part, 2, g_r[HALF:], right)
        g_l = partial(part, -1)
        pass_on(part, 3, g_l[:HALF], left)
        kept.append((g_r[:HALF], g_l[HALF:]))
    for part in range(2):
        g_r, g_l = kept[part]
        pass_on(part, 4, g_r + rs_arrived(part, 0), right)
        pass_on(part, 5, g_l + rs_arrived(part, 1), left)
    for part in range(2):
        g_o = partial(part, 0)
        g_a = g_o[:HALF] + rs_arrived(part, 3)
        g_b = g_o[HALF:] + rs_arrived(part, 2)
        start = part * BLK
        OUT[start : start + HALF] = (g_a + rs_arrived(part, 4)).astype(BF16)
        OUT[start + HALF : start + BLK] = (g_b + rs_arrived(part, 5)).astype(BF16)
    store = pltpu.make_async_copy(OUT, gout, loc.at[4])
    store.start()
    att_own.wait()
    arrived(att.at[:, oth_col], as_.at[0], ar.at[0])
    for c, when in started:
        if when is None:
            c.wait_send()
        else:
            pl.when(when)(c.wait_send)
    store.wait()


def solution(mesh):
    nctx, nhead = mesh.shape["ctx"], mesh.shape["head"]

    def body(features, w_qkv, block_links, d_out):
        w = jnp.transpose(w_qkv, (1, 0, 2))
        any_spec = pl.BlockSpec(memory_space=pl.ANY)
        hbm_spec = pl.BlockSpec(memory_space=pltpu.HBM)
        dma = pltpu.SemaphoreType.DMA
        vmem = pltpu.VMEM
        return tuple(
            pl.pallas_call(
                functools.partial(kernel, nctx, nhead),
                out_shape=[
                    jax.ShapeDtypeStruct((SH, SH), BF16),
                    jax.ShapeDtypeStruct((SH, SH), BF16),
                ],
                in_specs=[hbm_spec] * 4,
                out_specs=[any_spec, any_spec],
                scratch_shapes=[
                    vmem((4, SH, SH), BF16),
                    vmem((3, 1024, SH), BF16),
                    vmem((3, SH, SH), F32),
                    vmem((4, 8, SH, HD), BF16),
                    vmem((4, SH, HD), BF16),
                    vmem((2, ROWS, SH), F32),
                    vmem((8 * SH, 2 * SH), F32),
                    vmem((8 * SH, 2 * SH), F32),
                    vmem((8 * SH, 2 * SH), BF16),
                    vmem((8 * SH, 2 * SH), BF16),
                    vmem((2 * SH, 8 * SH), BF16),
                    vmem((2 * SH, 8 * SH), BF16),
                    vmem((8, 2 * SH, SH), F32),
                    vmem((8, 2 * SH, SH), F32),
                    vmem((4, 1, 2 * SH), F32),
                    vmem((HD, 8 * SH), BF16),
                    vmem((HD, 8 * SH), BF16),
                    vmem((4, 8, 2 * SH), F32),
                    vmem((4, 8, 2 * SH), F32),
                    vmem((2, SH, HD), BF16),
                    vmem((3, SH, SH), BF16),
                    vmem((3, SH, HD), BF16),
                    vmem((2, 6, HALF, SH), BF16),
                    vmem((2, 6, HALF, SH), BF16),
                    vmem((SH, SH), BF16),
                    vmem((4, SH, SH), BF16),
                    vmem((4, SH, HD), BF16),
                    pltpu.SMEM((2, 9), jnp.int32),
                    dma((6,)),
                    dma((6,)),
                    dma((6,)),
                    dma((7,)),
                    dma((7,)),
                    dma((4, 7)),
                    dma((4, 8)),
                    dma((1,)),
                    dma((1,)),
                    dma((4,)),
                    dma((4,)),
                    dma((1,)),
                    dma((1,)),
                    dma((3, 2)),
                    dma((3, 2)),
                    dma((2, 6)),
                    dma((2, 6)),
                ],
                compiler_params=pltpu.CompilerParams(
                    collective_id=0,
                    has_side_effects=True,
                    vmem_limit_bytes=60 * 1024 * 1024,
                ),
            )(features, w, block_links, d_out)
        )

    return jax.shard_map(
        body,
        mesh=mesh,
        in_specs=(P("ctx", "head"), P(None, None, "head"), P("ctx", None), P("ctx", "head")),
        out_specs=(P("ctx", "head"), P("ctx", "head")),
        check_vma=False,
    )
```

```python
import functools
import math

import jax
import jax.numpy as jnp
from jax import lax
from jax.experimental import pallas as pl
from jax.experimental.pallas import tpu as pltpu
from jax.sharding import PartitionSpec as P

MESH = pl.DeviceIdType.MESH
BLK = 128
HD = 128
HALF = 64
SH = 256
SCALE = HD ** (-0.5)
C2 = SCALE * math.log2(math.e)
DEAD = -1e30
F32 = jnp.float32
BF16 = jnp.bfloat16
DO, K, V, Q = range(4)
PAD = 2
ROWS = 24
PAIRS = ((3, 4), (0, 7), (2, 5), (1, 6))
ORDER = (0, 2, 1, 3)
FAR = (-2, -1, 1, 2)
SOURCE = {0: (0, 1), 1: (1, 0), 2: (1, 1), 5: (2, 0), 6: (2, 1), 7: (3, 0)}


def dot(a, b):
    return jnp.dot(a, b, preferred_element_type=F32)


def dot_t(a, b):
    return lax.dot_general(a, b, (((1,), (1,)), ((), ())), preferred_element_type=F32)


def fold8(x, op):
    return op(x.reshape(x.shape[0] // 8, 8, x.shape[1]), axis=0)


def kernel(
    nctx,
    nhead,
    feat,
    w,
    links,
    dout,
    both,
    F,
    W,
    ACC,
    WIN,
    OTH,
    BQ,
    S,
    DP,
    PB,
    DSB,
    PK,
    TK,
    KS,
    KDP,
    MS,
    KT,
    VT,
    STO,
    STI,
    AST,
    GP,
    GST,
    RSO,
    RSI,
    OUT,
    FF,
    FO,
    LK,
    loc,
    xs,
    xr,
    fs,
    fr,
    ws,
    wr,
    bs,
    br,
    ss,
    sr,
    as_,
    ar,
    gs,
    gr,
    rs,
    rr,
):
    g = lax.axis_index("ctx")
    hx = lax.axis_index("head")
    core = lax.rem(g, 2)
    oth = 1 - core
    chip = g // 2
    nchip = nctx // 2
    has = {-1: chip > 0, -2: chip > 1, 1: chip < nchip - 1, 2: chip < nchip - 2}
    far_slot, far_oth = 7 * core, 7 * oth
    far_here = ((core == 0) & has[-2]) | ((core == 1) & has[2])
    far_there = ((core == 1) & has[-2]) | ((core == 0) & has[2])

    def at(distance, which):
        return (lax.rem(chip + distance + nchip, nchip) * 2 + which, hx)

    right = (g, lax.rem(hx + 1, nhead))
    left = (g, lax.rem(hx + nhead - 1, nhead))
    partner = at(0, oth)
    own_col = pl.ds(pl.multiple_of(core * HD, HD), HD)
    oth_col = pl.ds(pl.multiple_of(oth * HD, HD), HD)
    A, B = pl.ds(0, BLK), pl.ds(BLK, BLK)

    att, gout = both.at[0], both.at[1]
    load_l = pltpu.make_async_copy(links, LK, loc.at[5])
    load_l.start()
    barrier = pltpu.get_barrier_semaphore()
    for peer in (right, left, partner):
        pl.semaphore_signal(barrier, inc=1, device_id=peer, device_id_type=MESH)
    count = 3
    for d in (1, -1, 2, -2):
        count += 2 * has[d].astype(jnp.int32)

        @pl.when(has[d])
        def _():
            for which in (0, 1):
                pl.semaphore_signal(barrier, inc=1, device_id=at(d, which), device_id_type=MESH)

    load_f = pltpu.make_async_copy(feat, F.at[0], loc.at[0])
    load_f.start()
    load_w = pltpu.make_async_copy(w, W, loc.at[1])
    load_w.start()
    load_d = pltpu.make_async_copy(dout.at[:, own_col], WIN.at[DO, 3 + core], loc.at[2])
    load_d.start()

    for d, n, slots in ((-2, 0, (0,)), (-1, 1, (1, 2)), (1, 2, (5, 6)), (2, 3, (7,))):

        @pl.when(jnp.logical_not(has[d]))
        def _():
            for slot in slots:
                for kind in range(4):
                    WIN[kind, slot] = jnp.zeros((SH, HD), BF16)
            STI[n, 0:4] = jnp.zeros((4, 2 * SH), F32)
            STI[n, 4:8] = jnp.full((4, 2 * SH), DEAD, F32)

    base = chip * 4 - 6 - PAD
    row = lax.broadcasted_iota(jnp.int32, (ROWS, BLK), 0)
    load_l.wait()
    for r in range(2):
        live = None
        for j in range(9):
            entry = LK[r, j]
            hit = row == jnp.where(entry >= 0, entry - base, -1)
            live = hit if live is None else live | hit
        BQ[core, :, r * BLK : (r + 1) * BLK] = jnp.where(live, 0.0, DEAD).astype(F32)

    started = []

    def send(src, dst, s_sem, r_sem, to, when=None):
        c = pltpu.make_async_remote_copy(
            src_ref=src,
            dst_ref=dst,
            send_sem=s_sem,
            recv_sem=r_sem,
            device_id=to,
            device_id_type=MESH,
        )
        if when is None:
            c.start()
        else:
            pl.when(when)(c.start)
        started.append((c, when))

    def arrived(dst, s_sem, r_sem, when=None):
        c = pltpu.make_async_remote_copy(
            src_ref=dst,
            dst_ref=dst,
            send_sem=s_sem,
            recv_sem=r_sem,
            device_id=partner,
            device_id_type=MESH,
        )
        if when is None:
            c.wait_recv()
        else:
            pl.when(when)(c.wait_recv)

    near = {0: has[-2], 1: has[-1], 2: has[-1], 5: has[1], 6: has[1], 7: has[2]}

    def do_arrived(slot):
        when = near[slot] if isinstance(slot, int) else None
        arrived(WIN.at[DO, slot], ws.at[DO, 0], wr.at[DO, slot], when)

    KV, QQ = pl.ds(K, 2), pl.ds(Q, 1)

    def kvq_arrived(kinds, slot):
        kind = kinds.start
        arrived(WIN.at[kinds, slot], ws.at[kind, 0], wr.at[kind, slot], near[slot])

    def partner_arrived(kinds):
        kind = kinds.start
        arrived(WIN.at[kinds, 3 + oth], ws.at[kind, 0], wr.at[kind, 3 + oth])

    def spread_do():
        own, other = dout.at[:, own_col], dout.at[:, oth_col]
        for n, (d, slot) in enumerate(((1, 1 + core), (-1, 5 + core))):
            dst, r_sem = WIN.at[DO, slot], wr.at[DO, slot]
            send(own, dst, ws.at[DO, 1 + 2 * n], r_sem, at(d, core), has[d])
            send(other, dst, ws.at[DO, 2 + 2 * n], r_sem, at(d, oth), has[d])

    def spread(kinds):
        kind = kinds.start
        send(OTH.at[kinds], WIN.at[kinds, 3 + core], ws.at[kind, 0], wr.at[kind, 3 + core], partner)
        for n, (d, slot) in enumerate(((1, 1 + core), (-1, 5 + core))):
            for m, (src, to) in enumerate(((WIN.at[kinds, 3 + core], core), (OTH.at[kinds], oth))):
                send(src, WIN.at[kinds, slot], ws.at[kind, 1 + 2 * n + m], wr.at[kind, slot], at(d, to), has[d])

    def relay_do():
        for n, (d, slot, to) in enumerate(((1, 2, 0), (-1, 5, 7))):
            do_arrived(slot)
            both = has[1] & has[-1]
            send(WIN.at[DO, slot], WIN.at[DO, to], ws.at[DO, 5 + n], wr.at[DO, to], at(d, core), both)

    class Gather:
        def __init__(self, src, buf, s, r, when):
            self.src, self.buf, self.s, self.r, self.when = src, buf, s, r, when
            half = buf.shape[1] // 2
            self.low, self.high = pl.ds(0, half), pl.ds(half, half)

        def begin(self):
            src, buf, low, high = self.src, self.buf, self.low, self.high
            for n, slot, half, to in ((0, 1, low, right), (3, 2, high, left), (1, 1, high, right), (2, 2, low, left)):
                send(src.at[half], buf.at[slot, half], self.s.at[n], self.r.at[n], to, self.when)

        def wait(self, slot, half, n):
            arrived(self.buf.at[slot, half], self.s.at[n], self.r.at[n], self.when)

        def pass_right(self):
            buf, low = self.buf, self.low
            self.wait(1, low, 0)
            send(buf.at[1, low], buf.at[3, low], self.s.at[4], self.r.at[4], right, self.when)

        def pass_left(self):
            buf, high = self.buf, self.high
            self.wait(2, high, 3)
            send(buf.at[2, high], buf.at[3, high], self.s.at[5], self.r.at[5], left, self.when)

        def rest(self):
            self.wait(1, self.high, 1)
            self.wait(2, self.low, 2)

        def end(self):
            self.wait(3, self.low, 4)
            self.wait(3, self.high, 5)

    def w_rows(step):
        s = lax.rem(hx + step + nhead, nhead)
        return pl.ds(pl.multiple_of(s * SH, SH), SH)

    def project(buf, i):
        total = None
        for slot, step in ((0, 0), (1, -1), (2, 1)):
            part = dot(buf[slot], W[i, w_rows(step), :])
            total = part if total is None else total + part
        ACC[i, : buf.shape[1]] = total

    def projected(buf, i):
        full = (ACC[i, : buf.shape[1]] + dot(buf[3], W[i, w_rows(2), :])).astype(BF16)
        low, high = full[:, :HD], full[:, HD:]
        return jnp.where(core == 0, low, high), jnp.where(core == 0, high, low)

    pl.semaphore_wait(barrier, count)

    mine = Gather(feat, F, xs, xr, None)
    far = Gather(FF.at[0], FF, fs, fr, far_here)
    mine.begin()
    out_two = ((core == 1) & has[2]) | ((core == 0) & has[-2])
    send(feat, FF.at[0], fs.at[6], fr.at[6], at(jnp.where(core == 1, 2, -2), oth), out_two)
    send(BQ.at[core], BQ.at[core], bs.at[0], br.at[0], partner)
    send(dout.at[:, oth_col], WIN.at[DO, 3 + core], ws.at[DO, 0], wr.at[DO, 3 + core], partner)
    for tab in (PB, DSB):
        tab[:SH, SH:] = jnp.zeros((SH, SH), BF16)
        tab[7 * SH :, :SH] = jnp.zeros((SH, SH), BF16)
    for tab in (PK, TK):
        for pos, e in enumerate(ORDER):
            where = slice(7 * SH, 8 * SH) if e < 2 else slice(0, SH)
            tab[pos * BLK : (pos + 1) * BLK, where] = jnp.zeros((BLK, SH), BF16)
    load_f.wait()
    load_w.wait()
    mine.pass_right()
    spread_do()
    mine.pass_left()
    arrived(FF.at[0], fs.at[6], fr.at[6], far_here)
    far.begin()
    mine.rest()
    for i in range(3):
        project(F, i)
    mine.end()
    WIN[K, 3 + core], OTH[K] = projected(F, 1)
    WIN[V, 3 + core], OTH[V] = projected(F, 2)
    spread(KV)
    WIN[Q, 3 + core], OTH[Q] = projected(F, 0)
    early = len(started)
    spread(QQ)
    far.pass_right()
    far.pass_left()
    relay_do()

    partner_arrived(QQ)
    load_d.wait()
    do_arrived(3 + oth)
    arrived(BQ.at[oth], bs.at[0], br.at[0])

    def lanes(s):
        return {0: (0,), 7: (1,)}.get(s, (0, 1))

    def scores(pair):
        tops = [None, None]
        for s in pair:
            for half in lanes(s):
                cols = slice(half * SH, (half + 1) * SH)
                x = dot_t(WIN[K, s], WIN[Q, 3 + half]) * C2
                for b in range(2):
                    wb = 2 * s + b + PAD
                    y = x[b * BLK : (b + 1) * BLK] + BQ[half, wb : wb + 1, :]
                    S[s * SH + b * BLK : s * SH + (b + 1) * BLK, cols] = y
                    top = fold8(y, jnp.max)
                    tops[half] = top if tops[half] is None else jnp.maximum(tops[half], top)
                DP[s * SH : (s + 1) * SH, cols] = dot_t(WIN[V, s], WIN[DO, 3 + half])
        return jnp.max(jnp.concatenate(tops, axis=1), axis=0, keepdims=True)

    def query_side(n, pair, m_old, l8, r8):
        m_new = jnp.maximum(m_old, scores(pair))
        MS[n] = m_new
        shrink = jnp.exp2(m_old - m_new)
        l8, r8 = l8 * shrink, r8 * shrink
        for s in pair:
            halves = lanes(s)
            cols = slice(halves[0] * SH, (halves[-1] + 1) * SH)
            step = 64 // len(halves)
            top = m_new[:, cols]

            def piece(i, carry):
                l, r = carry
                rows = pl.ds(pl.multiple_of(s * SH + i * step, step), step)
                e = jnp.exp2(S[rows, cols] - top)
                S[rows, cols] = e
                return l + fold8(e, jnp.sum), r + fold8(e * DP[rows, cols], jnp.sum)

            zero = jnp.zeros((8, SH * len(halves)), F32)
            l, r = lax.fori_loop(0, SH // step, piece, (zero, zero), unroll=2)
            if len(halves) == 1:
                pads = [jnp.zeros((8, SH), F32)] * 2
                pads[halves[0]] = l
                l = jnp.concatenate(pads, axis=1)
                pads[halves[0]] = r
                r = jnp.concatenate(pads, axis=1)
            l8, r8 = l8 + l, r8 + r
        return m_new, l8, r8

    partner_arrived(KV)
    m = jnp.full((1, 2 * SH), -3e38, F32)
    l8 = jnp.zeros((8, 2 * SH), F32)
    r8 = l8
    m, l8, r8 = query_side(0, PAIRS[0], m, l8, r8)

    far.rest()

    @pl.when(far_here)
    def _():
        for i in range(3):
            project(FF, i)

    far.end()

    @pl.when(far_here)
    def _():
        for kind, i in ((K, 1), (V, 2), (Q, 0)):
            WIN[kind, far_slot], FO[kind - 1] = projected(FF, i)

    kvq = pl.ds(K, 3)
    send(FO, WIN.at[kvq, far_slot], fs.at[7], fr.at[7], partner, far_here)
    arrived(WIN.at[kvq, far_oth], fs.at[7], fr.at[7], far_there)
    m, l8, r8 = query_side(1, PAIRS[1], m, l8, r8)
    for n in (2, 3):
        for s in PAIRS[n]:
            kvq_arrived(KV, s)
        m, l8, r8 = query_side(n, PAIRS[n], m, l8, r8)

    il = 1.0 / jnp.sum(l8, axis=0, keepdims=True)
    rd = jnp.sum(r8, axis=0, keepdims=True) * il
    for n, d in enumerate(FAR):
        STO[n, 0:1, :] = m
        STO[n, 1:2, :] = il
        STO[n, 2:3, :] = rd
        first = 6 + PAD + 4 * d
        for half in range(2):
            STO[n, 4:8, half * SH : (half + 1) * SH] = BQ[half, first : first + 4, :]
        send(STO.at[n], STI.at[3 - n], ss.at[n], sr.at[3 - n], at(d, core), has[d])

    for n, pair in enumerate(PAIRS):
        factor = jnp.exp2(MS[n] - m) * il
        for s in pair:
            halves = lanes(s)
            cols = slice(halves[0] * SH, (halves[-1] + 1) * SH)
            step = 64 // len(halves)
            f, r0 = factor[:, cols], rd[:, cols]

            def piece(i, carry):
                rows = pl.ds(pl.multiple_of(s * SH + i * step, step), step)
                p = S[rows, cols] * f
                PB[rows, cols] = p.astype(BF16)
                DSB[rows, cols] = (p * (DP[rows, cols] - r0)).astype(BF16)
                return carry

            lax.fori_loop(0, SH // step, piece, 0, unroll=2)
    for s in range(8):
        KT[:, s * SH : (s + 1) * SH] = WIN[K, s].T
        VT[:, s * SH : (s + 1) * SH] = WIN[V, s].T
    out = dot(VT[...], PB[...]).T.astype(BF16)
    AST[0] = out[:SH]
    AST[1] = out[SH:]
    send(AST.at[oth], att.at[:, own_col], as_.at[0], ar.at[0], partner)
    att_own = pltpu.make_async_copy(AST.at[core], att.at[:, own_col], loc.at[3])
    att_own.start()

    def hand_over(i, rows, low, high):
        GP[i, rows, own_col] = jnp.where(core == 0, low, high)
        GST[i, rows] = jnp.where(core == 0, high, low)

    def hand_on(kinds, n, rows):
        send(GST.at[kinds, rows], GP.at[kinds, rows, own_col], gs.at[n], gr.at[n], partner)

    dq = (dot(KT[...], DSB[...]) * SCALE).T.astype(BF16)
    every = pl.ds(0, SH)
    hand_over(0, every, dq[:SH], dq[SH:])
    hand_on(pl.ds(0, 1), 0, every)

    for pos, e in enumerate(ORDER):
        rows, keys = slice(pos * BLK, (pos + 1) * BLK), slice((6 + e) * BLK, (7 + e) * BLK)
        PK[rows, 3 * SH : 5 * SH] = PB[keys, :]
        TK[rows, 3 * SH : 5 * SH] = DSB[keys, :]

    def spans(s):
        return {0: (0,), 7: (1,)}.get(s, (0, 1))

    def wait_sent(copies):
        for c, when in copies:
            if when is None:
                c.wait_send()
            else:
                pl.when(when)(c.wait_send)

    wait_sent(started[:early])
    for s in (0, 7, 2, 5, 1, 6):
        if s in (1, 6, 0, 7):
            do_arrived(s)
        if s in (1, 2, 5, 6):
            kvq_arrived(QQ, s)
        for c in spans(s):
            rows = slice(c * SH, (c + 1) * SH)
            KS[s, rows] = dot_t(WIN[K, 3 + c], WIN[Q, s]) * C2
            KDP[s, rows] = dot_t(WIN[V, 3 + c], WIN[DO, s])
    for n, d in enumerate(FAR):
        arrived(STI.at[n], ss.at[n], sr.at[n], has[d])
    wide = (8 * SH, HD)
    for part in range(2):
        for s in (2, 5, 1, 6, 0, 7):
            n, half = SOURCE[s]
            cols = slice(half * SH, (half + 1) * SH)
            sm, sil, srd = (STI[n, i : i + 1, cols] for i in range(3))
            for c in spans(s):
                e = 2 * c + part
                pos = 2 * part + c
                shift = STI[n, 4 + e : 5 + e, cols] - sm

                def piece(i, carry):
                    src = pl.ds(pl.multiple_of(e * BLK + i * 64, 64), 64)
                    dst = pl.ds(pl.multiple_of(pos * BLK + i * 64, 64), 64)
                    p = jnp.exp2(KS[s, src] + shift) * sil
                    PK[dst, s * SH : (s + 1) * SH] = p.astype(BF16)
                    TK[dst, s * SH : (s + 1) * SH] = (p * (KDP[s, src] - srd)).astype(BF16)
                    return carry

                lax.fori_loop(0, BLK // 64, piece, 0, unroll=True)
        rows = slice(part * SH, (part + 1) * SH)
        dk = (dot(TK[rows, :], WIN[Q].reshape(wide)) * SCALE).astype(BF16)
        half = pl.ds(part * BLK, BLK)
        hand_over(1, half, dk[:BLK], dk[BLK:])
        dv = dot(PK[rows, :], WIN[DO].reshape(wide)).astype(BF16)
        hand_over(2, half, dv[:BLK], dv[BLK:])
        hand_on(pl.ds(1, 2), 1 + part, half)

    def partial(part, step):
        rows = w_rows(step)
        mine = slice(part * BLK, (part + 1) * BLK)
        return sum(dot_t(GP[i, mine, :], W[i, rows, :]) for i in range(3))

    def pass_on(part, n, value, to):
        RSO[part, n] = value.astype(BF16)
        send(RSO.at[part, n], RSI.at[part, n], rs.at[part, n], rr.at[part, n], to)

    def rs_arrived(part, n):
        arrived(RSI.at[part, n], rs.at[part, n], rr.at[part, n])
        return RSI[part, n].astype(F32)

    kept = []
    for part in range(2):
        if part == 0:
            arrived(GP.at[pl.ds(0, 1), every, oth_col], gs.at[0], gr.at[0])
        rows = pl.ds(part * BLK, BLK)
        arrived(GP.at[pl.ds(1, 2), rows, oth_col], gs.at[1 + part], gr.at[1 + part])
        gx = partial(part, 2)
        pass_on(part, 0, gx[:HALF], right)
        pass_on(part, 1, gx[HALF:], left)
        g_r = partial(part, 1)
        pass_on(part, 2, g_r[HALF:], right)
        g_l = partial(part, -1)
        pass_on(part, 3, g_l[:HALF], left)
        kept.append((g_r[:HALF], g_l[HALF:]))
    for part in range(2):
        g_r, g_l = kept[part]
        pass_on(part, 4, g_r + rs_arrived(part, 0), right)
        pass_on(part, 5, g_l + rs_arrived(part, 1), left)
    for part in range(2):
        g_o = partial(part, 0)
        g_a = g_o[:HALF] + rs_arrived(part, 3)
        g_b = g_o[HALF:] + rs_arrived(part, 2)
        start = part * BLK
        OUT[start : start + HALF] = (g_a + rs_arrived(part, 4)).astype(BF16)
        OUT[start + HALF : start + BLK] = (g_b + rs_arrived(part, 5)).astype(BF16)
    store = pltpu.make_async_copy(OUT, gout, loc.at[4])
    store.start()
    att_own.wait()
    arrived(att.at[:, oth_col], as_.at[0], ar.at[0])
    wait_sent(started[early:])
    store.wait()


def solution(mesh):
    nctx, nhead = mesh.shape["ctx"], mesh.shape["head"]

    def body(features, w_qkv, block_links, d_out):
        w = jnp.transpose(w_qkv, (1, 0, 2))
        any_spec = pl.BlockSpec(memory_space=pl.ANY)
        hbm_spec = pl.BlockSpec(memory_space=pltpu.HBM)
        dma = pltpu.SemaphoreType.DMA
        vmem = pltpu.VMEM
        out = (
            pl.pallas_call(
                functools.partial(kernel, nctx, nhead),
                out_shape=jax.ShapeDtypeStruct((2, SH, SH), BF16),
                in_specs=[hbm_spec] * 4,
                out_specs=any_spec,
                scratch_shapes=[
                    vmem((4, SH, SH), BF16),
                    vmem((3, 1024, SH), BF16),
                    vmem((3, SH, SH), F32),
                    vmem((4, 8, SH, HD), BF16),
                    vmem((4, SH, HD), BF16),
                    vmem((2, ROWS, SH), F32),
                    vmem((8 * SH, 2 * SH), F32),
                    vmem((8 * SH, 2 * SH), F32),
                    vmem((8 * SH, 2 * SH), BF16),
                    vmem((8 * SH, 2 * SH), BF16),
                    vmem((2 * SH, 8 * SH), BF16),
                    vmem((2 * SH, 8 * SH), BF16),
                    vmem((8, 2 * SH, SH), F32),
                    vmem((8, 2 * SH, SH), F32),
                    vmem((4, 1, 2 * SH), F32),
                    vmem((HD, 8 * SH), BF16),
                    vmem((HD, 8 * SH), BF16),
                    vmem((4, 8, 2 * SH), F32),
                    vmem((4, 8, 2 * SH), F32),
                    vmem((2, SH, HD), BF16),
                    vmem((3, SH, SH), BF16),
                    vmem((3, SH, HD), BF16),
                    vmem((2, 6, HALF, SH), BF16),
                    vmem((2, 6, HALF, SH), BF16),
                    vmem((SH, SH), BF16),
                    vmem((4, SH, SH), BF16),
                    vmem((3, SH, HD), BF16),
                    pltpu.SMEM((2, 9), jnp.int32),
                    dma((6,)),
                    dma((6,)),
                    dma((6,)),
                    dma((8,)),
                    dma((8,)),
                    dma((4, 7)),
                    dma((4, 8)),
                    dma((1,)),
                    dma((1,)),
                    dma((4,)),
                    dma((4,)),
                    dma((1,)),
                    dma((1,)),
                    dma((3,)),
                    dma((3,)),
                    dma((2, 6)),
                    dma((2, 6)),
                ],
                compiler_params=pltpu.CompilerParams(
                    collective_id=0,
                    has_side_effects=True,
                    vmem_limit_bytes=60 * 1024 * 1024,
                ),
            )(features, w, block_links, d_out)
        )
        return out[0], out[1]

    return jax.shard_map(
        body,
        mesh=mesh,
        in_specs=(P("ctx", "head"), P(None, None, "head"), P("ctx", None), P("ctx", "head")),
        out_specs=(P("ctx", "head"), P("ctx", "head")),
        check_vma=False,
    )
```

```python
import functools
import math

import jax
import jax.numpy as jnp
from jax import lax
from jax.experimental import pallas as pl
from jax.experimental.pallas import tpu as pltpu
from jax.sharding import PartitionSpec as P

MESH = pl.DeviceIdType.MESH
BLK = 128
HD = 128
HALF = 64
SH = 256
SCALE = HD ** (-0.5)
C2 = SCALE * math.log2(math.e)
DEAD = -1e30
F32 = jnp.float32
BF16 = jnp.bfloat16
DO, K, V, Q = range(4)
PAD = 2
ROWS = 24
PAIRS = ((3, 4), (0, 7), (2, 5), (1, 6))
ORDER = (0, 2, 1, 3)
FAR = (-2, -1, 1, 2)
SOURCE = {0: (0, 1), 1: (1, 0), 2: (1, 1), 5: (2, 0), 6: (2, 1), 7: (3, 0)}


def dot(a, b):
    return jnp.dot(a, b, preferred_element_type=F32)


def dot_t(a, b):
    return lax.dot_general(a, b, (((1,), (1,)), ((), ())), preferred_element_type=F32)


def fold8(x, op):
    return op(x.reshape(x.shape[0] // 8, 8, x.shape[1]), axis=0)


def kernel(
    nctx,
    nhead,
    feat,
    w,
    links,
    dout,
    both,
    F,
    W,
    ACC,
    WIN,
    OTH,
    BQ,
    S,
    DP,
    PB,
    DSB,
    PK,
    TK,
    KS,
    KDP,
    MS,
    KT,
    VT,
    STO,
    STI,
    DKV,
    AST,
    GP,
    GST,
    RSO,
    RSI,
    OUT,
    FF,
    FO,
    LK,
    loc,
    xs,
    xr,
    fs,
    fr,
    ws,
    wr,
    bs,
    br,
    ss,
    sr,
    as_,
    ar,
    gs,
    gr,
    rs,
    rr,
):
    g = lax.axis_index("ctx")
    hx = lax.axis_index("head")
    core = lax.rem(g, 2)
    oth = 1 - core
    chip = g // 2
    nchip = nctx // 2
    has = {-1: chip > 0, -2: chip > 1, 1: chip < nchip - 1, 2: chip < nchip - 2}
    far_slot, far_oth = 7 * core, 7 * oth
    far_here = ((core == 0) & has[-2]) | ((core == 1) & has[2])
    far_there = ((core == 1) & has[-2]) | ((core == 0) & has[2])

    def at(distance, which):
        return (lax.rem(chip + distance + nchip, nchip) * 2 + which, hx)

    right = (g, lax.rem(hx + 1, nhead))
    left = (g, lax.rem(hx + nhead - 1, nhead))
    partner = at(0, oth)
    own_col = pl.ds(pl.multiple_of(core * HD, HD), HD)
    oth_col = pl.ds(pl.multiple_of(oth * HD, HD), HD)
    A, B = pl.ds(0, BLK), pl.ds(BLK, BLK)

    att, gout = both.at[0], both.at[1]
    barrier = pltpu.get_barrier_semaphore()
    for peer in (right, left, partner):
        pl.semaphore_signal(barrier, inc=1, device_id=peer, device_id_type=MESH)
    count = 3
    for d in (1, -1, 2, -2):
        count += 2 * has[d].astype(jnp.int32)

        @pl.when(has[d])
        def _():
            for which in (0, 1):
                pl.semaphore_signal(barrier, inc=1, device_id=at(d, which), device_id_type=MESH)

    load_l = pltpu.make_async_copy(links, LK, loc.at[5])
    load_l.start()
    load_f = pltpu.make_async_copy(feat, F.at[0], loc.at[0])
    load_f.start()
    load_w = pltpu.make_async_copy(w, W, loc.at[1])
    load_w.start()
    load_d = pltpu.make_async_copy(dout.at[:, own_col], WIN.at[DO, 3 + core], loc.at[2])
    load_d.start()

    started = []

    def send(src, dst, s_sem, r_sem, to, when=None):
        c = pltpu.make_async_remote_copy(
            src_ref=src,
            dst_ref=dst,
            send_sem=s_sem,
            recv_sem=r_sem,
            device_id=to,
            device_id_type=MESH,
        )
        if when is None:
            c.start()
        else:
            pl.when(when)(c.start)
        started.append((c, when))

    def arrived(dst, s_sem, r_sem, when=None):
        c = pltpu.make_async_remote_copy(
            src_ref=dst,
            dst_ref=dst,
            send_sem=s_sem,
            recv_sem=r_sem,
            device_id=partner,
            device_id_type=MESH,
        )
        if when is None:
            c.wait_recv()
        else:
            pl.when(when)(c.wait_recv)

    near = {0: has[-2], 1: has[-1], 2: has[-1], 5: has[1], 6: has[1], 7: has[2]}

    def do_arrived(slot):
        when = near[slot] if isinstance(slot, int) else None
        arrived(WIN.at[DO, slot], ws.at[DO, 0], wr.at[DO, slot], when)

    KV, QQ = pl.ds(K, 2), pl.ds(Q, 1)

    def kvq_arrived(kinds, slot):
        kind = kinds.start
        arrived(WIN.at[kinds, slot], ws.at[kind, 0], wr.at[kind, slot], near[slot])

    def partner_arrived(kinds):
        kind = kinds.start
        arrived(WIN.at[kinds, 3 + oth], ws.at[kind, 0], wr.at[kind, 3 + oth])

    def spread_do():
        own, other = dout.at[:, own_col], dout.at[:, oth_col]
        for n, (d, slot) in enumerate(((1, 1 + core), (-1, 5 + core))):
            dst, r_sem = WIN.at[DO, slot], wr.at[DO, slot]
            send(own, dst, ws.at[DO, 1 + 2 * n], r_sem, at(d, core), has[d])
            send(other, dst, ws.at[DO, 2 + 2 * n], r_sem, at(d, oth), has[d])

    def spread(kinds):
        kind = kinds.start
        send(OTH.at[kinds], WIN.at[kinds, 3 + core], ws.at[kind, 0], wr.at[kind, 3 + core], partner)
        for n, (d, slot) in enumerate(((1, 1 + core), (-1, 5 + core))):
            for m, (src, to) in enumerate(((WIN.at[kinds, 3 + core], core), (OTH.at[kinds], oth))):
                send(src, WIN.at[kinds, slot], ws.at[kind, 1 + 2 * n + m], wr.at[kind, slot], at(d, to), has[d])

    def relay_do():
        for n, (d, slot, to) in enumerate(((1, 2, 0), (-1, 5, 7))):
            do_arrived(slot)
            both = has[1] & has[-1]
            send(WIN.at[DO, slot], WIN.at[DO, to], ws.at[DO, 5 + n], wr.at[DO, to], at(d, core), both)

    class Gather:
        def __init__(self, src, buf, s, r, when):
            self.src, self.buf, self.s, self.r, self.when = src, buf, s, r, when
            half = buf.shape[1] // 2
            self.low, self.high = pl.ds(0, half), pl.ds(half, half)

        def begin(self):
            src, buf, low, high = self.src, self.buf, self.low, self.high
            for n, slot, half, to in ((0, 1, low, right), (3, 2, high, left), (1, 1, high, right), (2, 2, low, left)):
                send(src.at[half], buf.at[slot, half], self.s.at[n], self.r.at[n], to, self.when)

        def wait(self, slot, half, n):
            arrived(self.buf.at[slot, half], self.s.at[n], self.r.at[n], self.when)

        def pass_right(self):
            buf, low = self.buf, self.low
            self.wait(1, low, 0)
            send(buf.at[1, low], buf.at[3, low], self.s.at[4], self.r.at[4], right, self.when)

        def pass_left(self):
            buf, high = self.buf, self.high
            self.wait(2, high, 3)
            send(buf.at[2, high], buf.at[3, high], self.s.at[5], self.r.at[5], left, self.when)

        def rest(self):
            self.wait(1, self.high, 1)
            self.wait(2, self.low, 2)

        def end(self):
            self.wait(3, self.low, 4)
            self.wait(3, self.high, 5)

    def w_rows(step):
        s = lax.rem(hx + step + nhead, nhead)
        return pl.ds(pl.multiple_of(s * SH, SH), SH)

    def project(buf, i):
        total = None
        for slot, step in ((0, 0), (1, -1), (2, 1)):
            part = dot(buf[slot], W[i, w_rows(step), :])
            total = part if total is None else total + part
        ACC[i, : buf.shape[1]] = total

    def projected(buf, i):
        full = (ACC[i, : buf.shape[1]] + dot(buf[3], W[i, w_rows(2), :])).astype(BF16)
        low, high = full[:, :HD], full[:, HD:]
        return jnp.where(core == 0, low, high), jnp.where(core == 0, high, low)

    pl.semaphore_wait(barrier, count)

    mine = Gather(feat, F, xs, xr, None)
    far = Gather(FF.at[0], FF, fs, fr, far_here)
    mine.begin()
    out_two = ((core == 1) & has[2]) | ((core == 0) & has[-2])
    send(feat, FF.at[0], fs.at[6], fr.at[6], at(jnp.where(core == 1, 2, -2), oth), out_two)
    send(dout.at[:, oth_col], WIN.at[DO, 3 + core], ws.at[DO, 0], wr.at[DO, 3 + core], partner)
    for d, n, slots in ((-2, 0, (0,)), (-1, 1, (1, 2)), (1, 2, (5, 6)), (2, 3, (7,))):

        @pl.when(jnp.logical_not(has[d]))
        def _():
            for slot in slots:
                for kind in range(4):
                    WIN[kind, slot] = jnp.zeros((SH, HD), BF16)
            STI[n, 0:4] = jnp.zeros((4, 2 * SH), F32)
            STI[n, 4:8] = jnp.full((4, 2 * SH), DEAD, F32)

    base = chip * 4 - 6 - PAD
    row = lax.broadcasted_iota(jnp.int32, (ROWS, BLK), 0)
    load_l.wait()
    for r in range(2):
        live = None
        for j in range(9):
            entry = LK[r, j]
            hit = row == jnp.where(entry >= 0, entry - base, -1)
            live = hit if live is None else live | hit
        BQ[core, :, r * BLK : (r + 1) * BLK] = jnp.where(live, 0.0, DEAD).astype(F32)

    send(BQ.at[core], BQ.at[core], bs.at[0], br.at[0], partner)
    for tab in (PB, DSB):
        tab[:SH, SH:] = jnp.zeros((SH, SH), BF16)
        tab[7 * SH :, :SH] = jnp.zeros((SH, SH), BF16)
    for tab in (PK, TK):
        for pos, e in enumerate(ORDER):
            where = slice(7 * SH, 8 * SH) if e < 2 else slice(0, SH)
            tab[pos * BLK : (pos + 1) * BLK, where] = jnp.zeros((BLK, SH), BF16)
    load_f.wait()
    load_w.wait()
    mine.pass_right()
    spread_do()
    mine.pass_left()
    arrived(FF.at[0], fs.at[6], fr.at[6], far_here)
    far.begin()
    mine.rest()
    for i in range(3):
        project(F, i)
    mine.end()
    WIN[K, 3 + core], OTH[K] = projected(F, 1)
    WIN[V, 3 + core], OTH[V] = projected(F, 2)
    spread(KV)
    WIN[Q, 3 + core], OTH[Q] = projected(F, 0)
    early = len(started)
    spread(QQ)
    far.pass_right()
    far.pass_left()

    partner_arrived(QQ)
    load_d.wait()
    do_arrived(3 + oth)
    arrived(BQ.at[oth], bs.at[0], br.at[0])

    def lanes(s):
        return {0: (0,), 7: (1,)}.get(s, (0, 1))

    def scores(pair):
        tops = [None, None]
        for s in pair:
            for half in lanes(s):
                cols = slice(half * SH, (half + 1) * SH)
                x = dot_t(WIN[K, s], WIN[Q, 3 + half]) * C2
                for b in range(2):
                    wb = 2 * s + b + PAD
                    y = x[b * BLK : (b + 1) * BLK] + BQ[half, wb : wb + 1, :]
                    S[s * SH + b * BLK : s * SH + (b + 1) * BLK, cols] = y
                    top = fold8(y, jnp.max)
                    tops[half] = top if tops[half] is None else jnp.maximum(tops[half], top)
                DP[s * SH : (s + 1) * SH, cols] = dot_t(WIN[V, s], WIN[DO, 3 + half])
        return jnp.max(jnp.concatenate(tops, axis=1), axis=0, keepdims=True)

    def query_side(n, pair, m_old, l8, r8):
        m_new = jnp.maximum(m_old, scores(pair))
        MS[n] = m_new
        shrink = jnp.exp2(m_old - m_new)
        l8, r8 = l8 * shrink, r8 * shrink
        for s in pair:
            halves = lanes(s)
            cols = slice(halves[0] * SH, (halves[-1] + 1) * SH)
            step = 64 // len(halves)
            top = m_new[:, cols]

            def piece(i, carry):
                l, r = carry
                rows = pl.ds(pl.multiple_of(s * SH + i * step, step), step)
                e = jnp.exp2(S[rows, cols] - top)
                S[rows, cols] = e
                return l + fold8(e, jnp.sum), r + fold8(e * DP[rows, cols], jnp.sum)

            zero = jnp.zeros((8, SH * len(halves)), F32)
            l, r = lax.fori_loop(0, SH // step, piece, (zero, zero), unroll=2)
            if len(halves) == 1:
                pads = [jnp.zeros((8, SH), F32)] * 2
                pads[halves[0]] = l
                l = jnp.concatenate(pads, axis=1)
                pads[halves[0]] = r
                r = jnp.concatenate(pads, axis=1)
            l8, r8 = l8 + l, r8 + r
        return m_new, l8, r8

    partner_arrived(KV)
    m = jnp.full((1, 2 * SH), -3e38, F32)
    l8 = jnp.zeros((8, 2 * SH), F32)
    r8 = l8
    m, l8, r8 = query_side(0, PAIRS[0], m, l8, r8)

    relay_do()
    far.rest()

    @pl.when(far_here)
    def _():
        for i in range(3):
            project(FF, i)

    far.end()

    @pl.when(far_here)
    def _():
        for kind, i in ((K, 1), (V, 2), (Q, 0)):
            WIN[kind, far_slot], FO[kind - 1] = projected(FF, i)

    kvq = pl.ds(K, 3)
    send(FO, WIN.at[kvq, far_slot], fs.at[7], fr.at[7], partner, far_here)
    arrived(WIN.at[kvq, far_oth], fs.at[7], fr.at[7], far_there)
    m, l8, r8 = query_side(1, PAIRS[1], m, l8, r8)
    for n in (2, 3):
        for s in PAIRS[n]:
            kvq_arrived(KV, s)
        m, l8, r8 = query_side(n, PAIRS[n], m, l8, r8)

    il = 1.0 / jnp.sum(l8, axis=0, keepdims=True)
    rd = jnp.sum(r8, axis=0, keepdims=True) * il
    for n, d in enumerate(FAR):
        STO[n, 0:1, :] = m
        STO[n, 1:2, :] = il
        STO[n, 2:3, :] = rd
        first = 6 + PAD + 4 * d
        for half in range(2):
            STO[n, 4:8, half * SH : (half + 1) * SH] = BQ[half, first : first + 4, :]
        send(STO.at[n], STI.at[3 - n], ss.at[n], sr.at[3 - n], at(d, core), has[d])

    for n, pair in enumerate(PAIRS):
        factor = jnp.exp2(MS[n] - m) * il
        for s in pair:
            halves = lanes(s)
            cols = slice(halves[0] * SH, (halves[-1] + 1) * SH)
            step = 64 // len(halves)
            f, r0 = factor[:, cols], rd[:, cols]

            def piece(i, carry):
                rows = pl.ds(pl.multiple_of(s * SH + i * step, step), step)
                p = S[rows, cols] * f
                PB[rows, cols] = p.astype(BF16)
                DSB[rows, cols] = (p * (DP[rows, cols] - r0)).astype(BF16)
                return carry

            lax.fori_loop(0, SH // step, piece, 0, unroll=2)
    for s in range(8):
        KT[:, s * SH : (s + 1) * SH] = WIN[K, s].T
        VT[:, s * SH : (s + 1) * SH] = WIN[V, s].T
    out = dot(VT[...], PB[...]).T.astype(BF16)
    AST[0] = out[:SH]
    AST[1] = out[SH:]
    send(AST.at[oth], att.at[:, own_col], as_.at[0], ar.at[0], partner)
    att_own = pltpu.make_async_copy(AST.at[core], att.at[:, own_col], loc.at[3])
    att_own.start()

    def hand_over(i, rows, low, high):
        GP[i, rows, own_col] = jnp.where(core == 0, low, high)
        GST[i, rows] = jnp.where(core == 0, high, low)

    def hand_on(kinds, n, rows):
        send(GST.at[kinds, rows], GP.at[kinds, rows, own_col], gs.at[n], gr.at[n], partner)

    dq = (dot(KT[...], DSB[...]) * SCALE).T.astype(BF16)
    every = pl.ds(0, SH)
    hand_over(0, every, dq[:SH], dq[SH:])
    hand_on(pl.ds(0, 1), 0, every)

    own_q, own_d = WIN[Q, 3:5].reshape(2 * SH, HD), WIN[DO, 3:5].reshape(2 * SH, HD)
    for pos, e in enumerate(ORDER):
        rows, keys = slice(pos * BLK, (pos + 1) * BLK), slice((6 + e) * BLK, (7 + e) * BLK)
        DKV[0, rows] = dot(DSB[keys, :], own_q)
        DKV[1, rows] = dot(PB[keys, :], own_d)

    def spans(s):
        return {0: (0,), 7: (1,)}.get(s, (0, 1))

    def wait_sent(copies):
        for c, when in copies:
            if when is None:
                c.wait_send()
            else:
                pl.when(when)(c.wait_send)

    wait_sent(started[:early])
    for s in (0, 7, 2, 5, 1, 6):
        if s in (1, 6, 0, 7):
            do_arrived(s)
        if s in (1, 2, 5, 6):
            kvq_arrived(QQ, s)
        for c in spans(s):
            rows = slice(c * SH, (c + 1) * SH)
            KS[s, rows] = dot_t(WIN[K, 3 + c], WIN[Q, s]) * C2
            KDP[s, rows] = dot_t(WIN[V, 3 + c], WIN[DO, s])
    for n, d in enumerate(FAR):
        arrived(STI.at[n], ss.at[n], sr.at[n], has[d])
    for part in range(2):
        for s in (2, 5, 1, 6, 0, 7):
            n, half = SOURCE[s]
            cols = slice(half * SH, (half + 1) * SH)
            sm, sil, srd = (STI[n, i : i + 1, cols] for i in range(3))
            for c in spans(s):
                e = 2 * c + part
                pos = 2 * part + c
                shift = STI[n, 4 + e : 5 + e, cols] - sm

                def piece(i, carry):
                    src = pl.ds(pl.multiple_of(e * BLK + i * 64, 64), 64)
                    dst = pl.ds(pl.multiple_of(pos * BLK + i * 64, 64), 64)
                    p = jnp.exp2(KS[s, src] + shift) * sil
                    PK[dst, s * SH : (s + 1) * SH] = p.astype(BF16)
                    TK[dst, s * SH : (s + 1) * SH] = (p * (KDP[s, src] - srd)).astype(BF16)
                    return carry

                lax.fori_loop(0, BLK // 64, piece, 0, unroll=True)
        rows = slice(part * SH, (part + 1) * SH)
        lo, hi, side = slice(0, 3 * SH), slice(5 * SH, 8 * SH), (3 * SH, HD)
        dk = DKV[0, rows] + dot(TK[rows, lo], WIN[Q, :3].reshape(side)) + dot(TK[rows, hi], WIN[Q, 5:].reshape(side))
        dk = (dk * SCALE).astype(BF16)
        half = pl.ds(part * BLK, BLK)
        hand_over(1, half, dk[:BLK], dk[BLK:])
        dv = DKV[1, rows] + dot(PK[rows, lo], WIN[DO, :3].reshape(side)) + dot(PK[rows, hi], WIN[DO, 5:].reshape(side))
        dv = dv.astype(BF16)
        hand_over(2, half, dv[:BLK], dv[BLK:])
        hand_on(pl.ds(1, 2), 1 + part, half)

    def partial(part, step):
        rows = w_rows(step)
        mine = slice(part * BLK, (part + 1) * BLK)
        return sum(dot_t(GP[i, mine, :], W[i, rows, :]) for i in range(3))

    def pass_on(part, n, value, to):
        RSO[part, n] = value.astype(BF16)
        send(RSO.at[part, n], RSI.at[part, n], rs.at[part, n], rr.at[part, n], to)

    def rs_arrived(part, n):
        arrived(RSI.at[part, n], rs.at[part, n], rr.at[part, n])
        return RSI[part, n].astype(F32)

    kept = []
    for part in range(2):
        if part == 0:
            arrived(GP.at[pl.ds(0, 1), every, oth_col], gs.at[0], gr.at[0])
        rows = pl.ds(part * BLK, BLK)
        arrived(GP.at[pl.ds(1, 2), rows, oth_col], gs.at[1 + part], gr.at[1 + part])
        gx = partial(part, 2)
        pass_on(part, 0, gx[:HALF], right)
        pass_on(part, 1, gx[HALF:], left)
        g_r = partial(part, 1)
        pass_on(part, 2, g_r[HALF:], right)
        g_l = partial(part, -1)
        pass_on(part, 3, g_l[:HALF], left)
        kept.append((g_r[:HALF], g_l[HALF:]))
    for part in range(2):
        g_r, g_l = kept[part]
        pass_on(part, 4, g_r + rs_arrived(part, 0), right)
        pass_on(part, 5, g_l + rs_arrived(part, 1), left)
    for part in range(2):
        g_o = partial(part, 0)
        g_a = g_o[:HALF] + rs_arrived(part, 3)
        g_b = g_o[HALF:] + rs_arrived(part, 2)
        start = part * BLK
        OUT[start : start + HALF] = (g_a + rs_arrived(part, 4)).astype(BF16)
        OUT[start + HALF : start + BLK] = (g_b + rs_arrived(part, 5)).astype(BF16)
    store = pltpu.make_async_copy(OUT, gout, loc.at[4])
    store.start()
    att_own.wait()
    arrived(att.at[:, oth_col], as_.at[0], ar.at[0])
    wait_sent(started[early:])
    store.wait()


def solution(mesh):
    nctx, nhead = mesh.shape["ctx"], mesh.shape["head"]

    def body(features, w_qkv, block_links, d_out):
        w = jnp.transpose(w_qkv, (1, 0, 2))
        any_spec = pl.BlockSpec(memory_space=pl.ANY)
        hbm_spec = pl.BlockSpec(memory_space=pltpu.HBM)
        dma = pltpu.SemaphoreType.DMA
        vmem = pltpu.VMEM
        out = (
            pl.pallas_call(
                functools.partial(kernel, nctx, nhead),
                out_shape=jax.ShapeDtypeStruct((2, SH, SH), BF16),
                in_specs=[hbm_spec] * 4,
                out_specs=any_spec,
                scratch_shapes=[
                    vmem((4, SH, SH), BF16),
                    vmem((3, 1024, SH), BF16),
                    vmem((3, SH, SH), F32),
                    vmem((4, 8, SH, HD), BF16),
                    vmem((4, SH, HD), BF16),
                    vmem((2, ROWS, SH), F32),
                    vmem((8 * SH, 2 * SH), F32),
                    vmem((8 * SH, 2 * SH), F32),
                    vmem((8 * SH, 2 * SH), BF16),
                    vmem((8 * SH, 2 * SH), BF16),
                    vmem((2 * SH, 8 * SH), BF16),
                    vmem((2 * SH, 8 * SH), BF16),
                    vmem((8, 2 * SH, SH), F32),
                    vmem((8, 2 * SH, SH), F32),
                    vmem((4, 1, 2 * SH), F32),
                    vmem((HD, 8 * SH), BF16),
                    vmem((HD, 8 * SH), BF16),
                    vmem((4, 8, 2 * SH), F32),
                    vmem((4, 8, 2 * SH), F32),
                    vmem((2, 2 * SH, HD), F32),
                    vmem((2, SH, HD), BF16),
                    vmem((3, SH, SH), BF16),
                    vmem((3, SH, HD), BF16),
                    vmem((2, 6, HALF, SH), BF16),
                    vmem((2, 6, HALF, SH), BF16),
                    vmem((SH, SH), BF16),
                    vmem((4, SH, SH), BF16),
                    vmem((3, SH, HD), BF16),
                    pltpu.SMEM((2, 9), jnp.int32),
                    dma((6,)),
                    dma((6,)),
                    dma((6,)),
                    dma((8,)),
                    dma((8,)),
                    dma((4, 7)),
                    dma((4, 8)),
                    dma((1,)),
                    dma((1,)),
                    dma((4,)),
                    dma((4,)),
                    dma((1,)),
                    dma((1,)),
                    dma((3,)),
                    dma((3,)),
                    dma((2, 6)),
                    dma((2, 6)),
                ],
                compiler_params=pltpu.CompilerParams(
                    collective_id=0,
                    has_side_effects=True,
                    vmem_limit_bytes=60 * 1024 * 1024,
                ),
            )(features, w, block_links, d_out)
        )
        return out[0], out[1]

    return jax.shard_map(
        body,
        mesh=mesh,
        in_specs=(P("ctx", "head"), P(None, None, "head"), P("ctx", None), P("ctx", "head")),
        out_specs=(P("ctx", "head"), P("ctx", "head")),
        check_vma=False,
    )
```

```python
import functools
import math

import jax
import jax.numpy as jnp
from jax import lax
from jax.experimental import pallas as pl
from jax.experimental.pallas import tpu as pltpu
from jax.sharding import PartitionSpec as P

MESH = pl.DeviceIdType.MESH
BLK = 128
HD = 128
HALF = 64
SH = 256
SCALE = HD ** (-0.5)
C2 = SCALE * math.log2(math.e)
DEAD = -1e30
F32 = jnp.float32
BF16 = jnp.bfloat16
DO, K, V, Q = range(4)
PAD = 2
ROWS = 24
PAIRS = ((3, 4), (0, 7), (2, 5), (1, 6))
ORDER = (0, 2, 1, 3)
FAR = (-2, -1, 1, 2)
SOURCE = {0: (0, 1), 1: (1, 0), 2: (1, 1), 5: (2, 0), 6: (2, 1), 7: (3, 0)}


def dot(a, b):
    return jnp.dot(a, b, preferred_element_type=F32)


def dot_t(a, b):
    return lax.dot_general(a, b, (((1,), (1,)), ((), ())), preferred_element_type=F32)


def fold8(x, op):
    return op(x.reshape(x.shape[0] // 8, 8, x.shape[1]), axis=0)


def kernel(
    nctx,
    nhead,
    feat,
    w,
    links,
    dout,
    both,
    F,
    W,
    ACC,
    WIN,
    OTH,
    BQ,
    S,
    DP,
    PB,
    DSB,
    PK,
    TK,
    KS,
    KDP,
    MS,
    KT,
    VT,
    STO,
    STI,
    DKV,
    AST,
    GP,
    GST,
    RSO,
    RSI,
    OUT,
    FF,
    FO,
    LK,
    loc,
    xs,
    xr,
    fs,
    fr,
    ws,
    wr,
    bs,
    br,
    ss,
    sr,
    as_,
    ar,
    gs,
    gr,
    rs,
    rr,
):
    g = lax.axis_index("ctx")
    hx = lax.axis_index("head")
    core = lax.rem(g, 2)
    oth = 1 - core
    chip = g // 2
    nchip = nctx // 2
    has = {-1: chip > 0, -2: chip > 1, 1: chip < nchip - 1, 2: chip < nchip - 2}
    far_slot, far_oth = 7 * core, 7 * oth
    far_here = ((core == 0) & has[-2]) | ((core == 1) & has[2])
    far_there = ((core == 1) & has[-2]) | ((core == 0) & has[2])

    def at(distance, which):
        return (lax.rem(chip + distance + nchip, nchip) * 2 + which, hx)

    right = (g, lax.rem(hx + 1, nhead))
    left = (g, lax.rem(hx + nhead - 1, nhead))
    partner = at(0, oth)
    own_col = pl.ds(pl.multiple_of(core * HD, HD), HD)
    oth_col = pl.ds(pl.multiple_of(oth * HD, HD), HD)
    A, B = pl.ds(0, BLK), pl.ds(BLK, BLK)

    att, gout = both.at[0], both.at[1]
    barrier = pltpu.get_barrier_semaphore()
    for peer in (right, left, partner):
        pl.semaphore_signal(barrier, inc=1, device_id=peer, device_id_type=MESH)
    count = 3
    for d in (1, -1, 2, -2):
        count += 2 * has[d].astype(jnp.int32)

        @pl.when(has[d])
        def _():
            for which in (0, 1):
                pl.semaphore_signal(barrier, inc=1, device_id=at(d, which), device_id_type=MESH)

    load_l = pltpu.make_async_copy(links, LK, loc.at[5])
    load_l.start()
    load_f = pltpu.make_async_copy(feat, F.at[0], loc.at[0])
    load_f.start()
    load_w = pltpu.make_async_copy(w, W, loc.at[1])
    load_w.start()
    load_d = pltpu.make_async_copy(dout.at[:, own_col], WIN.at[DO, 3 + core], loc.at[2])
    load_d.start()

    started = []

    def send(src, dst, s_sem, r_sem, to, when=None):
        c = pltpu.make_async_remote_copy(
            src_ref=src,
            dst_ref=dst,
            send_sem=s_sem,
            recv_sem=r_sem,
            device_id=to,
            device_id_type=MESH,
        )
        if when is None:
            c.start()
        else:
            pl.when(when)(c.start)
        started.append((c, when))

    def arrived(dst, s_sem, r_sem, when=None):
        c = pltpu.make_async_remote_copy(
            src_ref=dst,
            dst_ref=dst,
            send_sem=s_sem,
            recv_sem=r_sem,
            device_id=partner,
            device_id_type=MESH,
        )
        if when is None:
            c.wait_recv()
        else:
            pl.when(when)(c.wait_recv)

    near = {0: has[-2], 1: has[-1], 2: has[-1], 5: has[1], 6: has[1], 7: has[2]}

    def do_arrived(slot):
        when = near[slot] if isinstance(slot, int) else None
        arrived(WIN.at[DO, slot], ws.at[DO, 0], wr.at[DO, slot], when)

    KV, QQ = pl.ds(K, 2), pl.ds(Q, 1)

    def kvq_arrived(kinds, slot):
        kind = kinds.start
        arrived(WIN.at[kinds, slot], ws.at[kind, 0], wr.at[kind, slot], near[slot])

    def partner_arrived(kinds):
        kind = kinds.start
        arrived(WIN.at[kinds, 3 + oth], ws.at[kind, 0], wr.at[kind, 3 + oth])

    def spread_do():
        own, other = dout.at[:, own_col], dout.at[:, oth_col]
        for n, (d, slot) in enumerate(((1, 1 + core), (-1, 5 + core))):
            dst, r_sem = WIN.at[DO, slot], wr.at[DO, slot]
            send(own, dst, ws.at[DO, 1 + 2 * n], r_sem, at(d, core), has[d])
            send(other, dst, ws.at[DO, 2 + 2 * n], r_sem, at(d, oth), has[d])

    def spread(kinds):
        kind = kinds.start
        send(OTH.at[kinds], WIN.at[kinds, 3 + core], ws.at[kind, 0], wr.at[kind, 3 + core], partner)
        for n, (d, slot) in enumerate(((1, 1 + core), (-1, 5 + core))):
            for m, (src, to) in enumerate(((WIN.at[kinds, 3 + core], core), (OTH.at[kinds], oth))):
                send(src, WIN.at[kinds, slot], ws.at[kind, 1 + 2 * n + m], wr.at[kind, slot], at(d, to), has[d])

    def relay_do():
        for n, (d, slot, to) in enumerate(((1, 2, 0), (-1, 5, 7))):
            do_arrived(slot)
            both = has[1] & has[-1]
            send(WIN.at[DO, slot], WIN.at[DO, to], ws.at[DO, 5 + n], wr.at[DO, to], at(d, core), both)

    class Gather:
        def __init__(self, src, buf, s, r, when):
            self.src, self.buf, self.s, self.r, self.when = src, buf, s, r, when
            half = buf.shape[1] // 2
            self.low, self.high = pl.ds(0, half), pl.ds(half, half)

        def begin(self):
            src, buf, low, high = self.src, self.buf, self.low, self.high
            for n, slot, half, to in ((0, 1, low, right), (3, 2, high, left), (1, 1, high, right), (2, 2, low, left)):
                send(src.at[half], buf.at[slot, half], self.s.at[n], self.r.at[n], to, self.when)

        def wait(self, slot, half, n):
            arrived(self.buf.at[slot, half], self.s.at[n], self.r.at[n], self.when)

        def pass_right(self):
            buf, low = self.buf, self.low
            self.wait(1, low, 0)
            send(buf.at[1, low], buf.at[3, low], self.s.at[4], self.r.at[4], right, self.when)

        def pass_left(self):
            buf, high = self.buf, self.high
            self.wait(2, high, 3)
            send(buf.at[2, high], buf.at[3, high], self.s.at[5], self.r.at[5], left, self.when)

        def rest(self):
            self.wait(1, self.high, 1)
            self.wait(2, self.low, 2)

        def end(self):
            self.wait(3, self.low, 4)
            self.wait(3, self.high, 5)

    def w_rows(step):
        s = lax.rem(hx + step + nhead, nhead)
        return pl.ds(pl.multiple_of(s * SH, SH), SH)

    def project(buf, i):
        total = None
        for slot, step in ((0, 0), (1, -1), (2, 1)):
            part = dot(buf[slot], W[i, w_rows(step), :])
            total = part if total is None else total + part
        ACC[i, : buf.shape[1]] = total

    def projected(buf, i):
        full = (ACC[i, : buf.shape[1]] + dot(buf[3], W[i, w_rows(2), :])).astype(BF16)
        low, high = full[:, :HD], full[:, HD:]
        return jnp.where(core == 0, low, high), jnp.where(core == 0, high, low)

    pl.semaphore_wait(barrier, count)

    mine = Gather(feat, F, xs, xr, None)
    far = Gather(FF.at[0], FF, fs, fr, far_here)
    mine.begin()
    out_two = ((core == 1) & has[2]) | ((core == 0) & has[-2])
    send(feat, FF.at[0], fs.at[6], fr.at[6], at(jnp.where(core == 1, 2, -2), oth), out_two)
    send(dout.at[:, oth_col], WIN.at[DO, 3 + core], ws.at[DO, 0], wr.at[DO, 3 + core], partner)
    for d, n, slots in ((-2, 0, (0,)), (-1, 1, (1, 2)), (1, 2, (5, 6)), (2, 3, (7,))):

        @pl.when(jnp.logical_not(has[d]))
        def _():
            for slot in slots:
                for kind in range(4):
                    WIN[kind, slot] = jnp.zeros((SH, HD), BF16)
            STI[n, 0:4] = jnp.zeros((4, 2 * SH), F32)
            STI[n, 4:8] = jnp.full((4, 2 * SH), DEAD, F32)

    base = chip * 4 - 6 - PAD
    row = lax.broadcasted_iota(jnp.int32, (ROWS, BLK), 0)
    load_l.wait()
    for r in range(2):
        live = None
        for j in range(9):
            entry = LK[r, j]
            hit = row == jnp.where(entry >= 0, entry - base, -1)
            live = hit if live is None else live | hit
        BQ[core, :, r * BLK : (r + 1) * BLK] = jnp.where(live, 0.0, DEAD).astype(F32)

    send(BQ.at[core], BQ.at[core], bs.at[0], br.at[0], partner)
    for tab in (PB, DSB):
        tab[:SH, SH:] = jnp.zeros((SH, SH), BF16)
        tab[7 * SH :, :SH] = jnp.zeros((SH, SH), BF16)
    for tab in (PK, TK):
        for pos, e in enumerate(ORDER):
            where = slice(7 * SH, 8 * SH) if e < 2 else slice(0, SH)
            tab[pos * BLK : (pos + 1) * BLK, where] = jnp.zeros((BLK, SH), BF16)
    load_f.wait()
    load_w.wait()
    mine.pass_right()
    spread_do()
    mine.pass_left()
    arrived(FF.at[0], fs.at[6], fr.at[6], far_here)
    far.begin()
    mine.rest()
    for i in range(3):
        project(F, i)
    mine.end()
    WIN[K, 3 + core], OTH[K] = projected(F, 1)
    WIN[V, 3 + core], OTH[V] = projected(F, 2)
    spread(KV)
    WIN[Q, 3 + core], OTH[Q] = projected(F, 0)
    early = len(started)
    spread(QQ)
    far.pass_right()
    far.pass_left()

    partner_arrived(QQ)
    load_d.wait()
    do_arrived(3 + oth)
    arrived(BQ.at[oth], bs.at[0], br.at[0])

    def lanes(s):
        return {0: (0,), 7: (1,)}.get(s, (0, 1))

    def scores(pair):
        tops = [None, None]
        for s in pair:
            for half in lanes(s):
                cols = slice(half * SH, (half + 1) * SH)
                x = dot_t(WIN[K, s], WIN[Q, 3 + half]) * C2
                for b in range(2):
                    wb = 2 * s + b + PAD
                    y = x[b * BLK : (b + 1) * BLK] + BQ[half, wb : wb + 1, :]
                    S[s * SH + b * BLK : s * SH + (b + 1) * BLK, cols] = y
                    top = fold8(y, jnp.max)
                    tops[half] = top if tops[half] is None else jnp.maximum(tops[half], top)
                DP[s * SH : (s + 1) * SH, cols] = dot_t(WIN[V, s], WIN[DO, 3 + half])
        return jnp.max(jnp.concatenate(tops, axis=1), axis=0, keepdims=True)

    def query_side(n, pair, m_old, l8, r8):
        m_new = jnp.maximum(m_old, scores(pair))
        MS[n] = m_new
        shrink = jnp.exp2(m_old - m_new)
        l8, r8 = l8 * shrink, r8 * shrink
        for s in pair:
            halves = lanes(s)
            cols = slice(halves[0] * SH, (halves[-1] + 1) * SH)
            step = 64 // len(halves)
            top = m_new[:, cols]

            def piece(i, carry):
                l, r = carry
                rows = pl.ds(pl.multiple_of(s * SH + i * step, step), step)
                e = jnp.exp2(S[rows, cols] - top)
                S[rows, cols] = e
                return l + fold8(e, jnp.sum), r + fold8(e * DP[rows, cols], jnp.sum)

            zero = jnp.zeros((8, SH * len(halves)), F32)
            l, r = lax.fori_loop(0, SH // step, piece, (zero, zero), unroll=2)
            if len(halves) == 1:
                pads = [jnp.zeros((8, SH), F32)] * 2
                pads[halves[0]] = l
                l = jnp.concatenate(pads, axis=1)
                pads[halves[0]] = r
                r = jnp.concatenate(pads, axis=1)
            l8, r8 = l8 + l, r8 + r
        return m_new, l8, r8

    partner_arrived(KV)
    m = jnp.full((1, 2 * SH), -3e38, F32)
    l8 = jnp.zeros((8, 2 * SH), F32)
    r8 = l8
    m, l8, r8 = query_side(0, PAIRS[0], m, l8, r8)

    relay_do()
    far.rest()

    @pl.when(far_here)
    def _():
        for i in range(3):
            project(FF, i)

    far.end()

    @pl.when(far_here)
    def _():
        for kind, i in ((K, 1), (V, 2), (Q, 0)):
            WIN[kind, far_slot], FO[kind - 1] = projected(FF, i)

    kvq = pl.ds(K, 3)
    send(FO, WIN.at[kvq, far_slot], fs.at[7], fr.at[7], partner, far_here)
    arrived(WIN.at[kvq, far_oth], fs.at[7], fr.at[7], far_there)
    m, l8, r8 = query_side(1, PAIRS[1], m, l8, r8)
    for n in (2, 3):
        for s in PAIRS[n]:
            kvq_arrived(KV, s)
        m, l8, r8 = query_side(n, PAIRS[n], m, l8, r8)

    il = 1.0 / jnp.sum(l8, axis=0, keepdims=True)
    rd = jnp.sum(r8, axis=0, keepdims=True) * il
    for n, d in enumerate(FAR):
        STO[n, 0:1, :] = m
        STO[n, 1:2, :] = il
        STO[n, 2:3, :] = rd
        first = 6 + PAD + 4 * d
        for half in range(2):
            STO[n, 4:8, half * SH : (half + 1) * SH] = BQ[half, first : first + 4, :]
        send(STO.at[n], STI.at[3 - n], ss.at[n], sr.at[3 - n], at(d, core), has[d])

    for n, pair in enumerate(PAIRS):
        factor = jnp.exp2(MS[n] - m) * il
        for s in pair:
            halves = lanes(s)
            cols = slice(halves[0] * SH, (halves[-1] + 1) * SH)
            step = 64 // len(halves)
            f, r0 = factor[:, cols], rd[:, cols]

            def piece(i, carry):
                rows = pl.ds(pl.multiple_of(s * SH + i * step, step), step)
                p = S[rows, cols] * f
                PB[rows, cols] = p.astype(BF16)
                DSB[rows, cols] = (p * (DP[rows, cols] - r0)).astype(BF16)
                return carry

            lax.fori_loop(0, SH // step, piece, 0, unroll=2)
    for s in range(8):
        KT[:, s * SH : (s + 1) * SH] = WIN[K, s].T
        VT[:, s * SH : (s + 1) * SH] = WIN[V, s].T
    out = dot(VT[...], PB[...]).T.astype(BF16)
    AST[0] = out[:SH]
    AST[1] = out[SH:]
    send(AST.at[oth], att.at[:, own_col], as_.at[0], ar.at[0], partner)
    att_own = pltpu.make_async_copy(AST.at[core], att.at[:, own_col], loc.at[3])
    att_own.start()

    def hand_over(i, rows, low, high):
        GP[i, rows, own_col] = jnp.where(core == 0, low, high)
        GST[i, rows] = jnp.where(core == 0, high, low)

    def hand_on(kinds, n, rows):
        send(GST.at[kinds, rows], GP.at[kinds, rows, own_col], gs.at[n], gr.at[n], partner)

    dq = (dot(KT[...], DSB[...]) * SCALE).T.astype(BF16)
    every = pl.ds(0, SH)
    hand_over(0, every, dq[:SH], dq[SH:])
    hand_on(pl.ds(0, 1), 0, every)

    own_q, own_d = WIN[Q, 3:5].reshape(2 * SH, HD), WIN[DO, 3:5].reshape(2 * SH, HD)
    for pos, e in enumerate(ORDER):
        rows, keys = slice(pos * BLK, (pos + 1) * BLK), slice((6 + e) * BLK, (7 + e) * BLK)
        DKV[0, rows] = dot(DSB[keys, :], own_q)
        DKV[1, rows] = dot(PB[keys, :], own_d)

    def spans(s):
        return {0: (0,), 7: (1,)}.get(s, (0, 1))

    def wait_sent(copies):
        for c, when in copies:
            if when is None:
                c.wait_send()
            else:
                pl.when(when)(c.wait_send)

    wait_sent(started[:early])
    for s in (0, 7, 2, 5, 1, 6):
        if s in (1, 6, 0, 7):
            do_arrived(s)
        if s in (1, 2, 5, 6):
            kvq_arrived(QQ, s)
        for c in spans(s):
            rows = slice(c * SH, (c + 1) * SH)
            KS[s, rows] = dot_t(WIN[K, 3 + c], WIN[Q, s]) * C2
            KDP[s, rows] = dot_t(WIN[V, 3 + c], WIN[DO, s])
    for n, d in enumerate(FAR):
        arrived(STI.at[n], ss.at[n], sr.at[n], has[d])
    for part in range(2):
        for s in (2, 5, 1, 6, 0, 7):
            n, half = SOURCE[s]
            cols = slice(half * SH, (half + 1) * SH)
            sm, sil, srd = (STI[n, i : i + 1, cols] for i in range(3))
            for c in spans(s):
                e = 2 * c + part
                pos = 2 * part + c
                shift = STI[n, 4 + e : 5 + e, cols] - sm

                def piece(i, carry):
                    src = pl.ds(pl.multiple_of(e * BLK + i * 64, 64), 64)
                    dst = pl.ds(pl.multiple_of(pos * BLK + i * 64, 64), 64)
                    p = jnp.exp2(KS[s, src] + shift) * sil
                    PK[dst, s * SH : (s + 1) * SH] = p.astype(BF16)
                    TK[dst, s * SH : (s + 1) * SH] = (p * (KDP[s, src] - srd)).astype(BF16)
                    return carry

                lax.fori_loop(0, BLK // 64, piece, 0, unroll=True)
        rows = slice(part * SH, (part + 1) * SH)
        lo, hi, side = slice(0, 3 * SH), slice(5 * SH, 8 * SH), (3 * SH, HD)
        dk = DKV[0, rows] + dot(TK[rows, lo], WIN[Q, :3].reshape(side)) + dot(TK[rows, hi], WIN[Q, 5:].reshape(side))
        dk = (dk * SCALE).astype(BF16)
        half = pl.ds(part * BLK, BLK)
        hand_over(1, half, dk[:BLK], dk[BLK:])
        dv = DKV[1, rows] + dot(PK[rows, lo], WIN[DO, :3].reshape(side)) + dot(PK[rows, hi], WIN[DO, 5:].reshape(side))
        dv = dv.astype(BF16)
        hand_over(2, half, dv[:BLK], dv[BLK:])
        hand_on(pl.ds(1, 2), 1 + part, half)

    def partial(part, step):
        rows = w_rows(step)
        mine = slice(part * BLK, (part + 1) * BLK)
        return sum(dot_t(GP[i, mine, :], W[i, rows, :]) for i in range(3))

    def pass_on(part, n, value, to):
        RSO[part, n] = value.astype(BF16)
        send(RSO.at[part, n], RSI.at[part, n], rs.at[part, n], rr.at[part, n], to)

    def rs_arrived(part, n):
        arrived(RSI.at[part, n], rs.at[part, n], rr.at[part, n])
        return RSI[part, n].astype(F32)

    kept = []
    stores = []
    for part in range(2):
        if part == 0:
            arrived(GP.at[pl.ds(0, 1), every, oth_col], gs.at[0], gr.at[0])
        rows = pl.ds(part * BLK, BLK)
        arrived(GP.at[pl.ds(1, 2), rows, oth_col], gs.at[1 + part], gr.at[1 + part])
        gx = partial(part, 2)
        pass_on(part, 0, gx[:HALF], right)
        pass_on(part, 1, gx[HALF:], left)
        g_r = partial(part, 1)
        pass_on(part, 2, g_r[HALF:], right)
        g_l = partial(part, -1)
        pass_on(part, 3, g_l[:HALF], left)
        kept.append((g_r[:HALF], g_l[HALF:]))
    for part in range(2):
        g_r, g_l = kept[part]
        pass_on(part, 4, g_r + rs_arrived(part, 0), right)
        pass_on(part, 5, g_l + rs_arrived(part, 1), left)
    for part in range(2):
        g_o = partial(part, 0)
        g_a = g_o[:HALF] + rs_arrived(part, 3)
        g_b = g_o[HALF:] + rs_arrived(part, 2)
        start = part * BLK
        OUT[start : start + HALF] = (g_a + rs_arrived(part, 4)).astype(BF16)
        OUT[start + HALF : start + BLK] = (g_b + rs_arrived(part, 5)).astype(BF16)
        rows = pl.ds(start, BLK)
        stores.append(pltpu.make_async_copy(OUT.at[rows], gout.at[rows], loc.at[6 + part]))
        stores[-1].start()
    att_own.wait()
    arrived(att.at[:, oth_col], as_.at[0], ar.at[0])
    wait_sent(started[early:])
    for store in stores:
        store.wait()


def solution(mesh):
    nctx, nhead = mesh.shape["ctx"], mesh.shape["head"]

    def body(features, w_qkv, block_links, d_out):
        w = jnp.transpose(w_qkv, (1, 0, 2))
        any_spec = pl.BlockSpec(memory_space=pl.ANY)
        hbm_spec = pl.BlockSpec(memory_space=pltpu.HBM)
        dma = pltpu.SemaphoreType.DMA
        vmem = pltpu.VMEM
        out = (
            pl.pallas_call(
                functools.partial(kernel, nctx, nhead),
                out_shape=jax.ShapeDtypeStruct((2, SH, SH), BF16),
                in_specs=[hbm_spec] * 4,
                out_specs=any_spec,
                scratch_shapes=[
                    vmem((4, SH, SH), BF16),
                    vmem((3, 1024, SH), BF16),
                    vmem((3, SH, SH), F32),
                    vmem((4, 8, SH, HD), BF16),
                    vmem((4, SH, HD), BF16),
                    vmem((2, ROWS, SH), F32),
                    vmem((8 * SH, 2 * SH), F32),
                    vmem((8 * SH, 2 * SH), F32),
                    vmem((8 * SH, 2 * SH), BF16),
                    vmem((8 * SH, 2 * SH), BF16),
                    vmem((2 * SH, 8 * SH), BF16),
                    vmem((2 * SH, 8 * SH), BF16),
                    vmem((8, 2 * SH, SH), F32),
                    vmem((8, 2 * SH, SH), F32),
                    vmem((4, 1, 2 * SH), F32),
                    vmem((HD, 8 * SH), BF16),
                    vmem((HD, 8 * SH), BF16),
                    vmem((4, 8, 2 * SH), F32),
                    vmem((4, 8, 2 * SH), F32),
                    vmem((2, 2 * SH, HD), F32),
                    vmem((2, SH, HD), BF16),
                    vmem((3, SH, SH), BF16),
                    vmem((3, SH, HD), BF16),
                    vmem((2, 6, HALF, SH), BF16),
                    vmem((2, 6, HALF, SH), BF16),
                    vmem((SH, SH), BF16),
                    vmem((4, SH, SH), BF16),
                    vmem((3, SH, HD), BF16),
                    pltpu.SMEM((2, 9), jnp.int32),
                    dma((8,)),
                    dma((6,)),
                    dma((6,)),
                    dma((8,)),
                    dma((8,)),
                    dma((4, 7)),
                    dma((4, 8)),
                    dma((1,)),
                    dma((1,)),
                    dma((4,)),
                    dma((4,)),
                    dma((1,)),
                    dma((1,)),
                    dma((3,)),
                    dma((3,)),
                    dma((2, 6)),
                    dma((2, 6)),
                ],
                compiler_params=pltpu.CompilerParams(
                    collective_id=0,
                    has_side_effects=True,
                    vmem_limit_bytes=60 * 1024 * 1024,
                ),
            )(features, w, block_links, d_out)
        )
        return out[0], out[1]

    return jax.shard_map(
        body,
        mesh=mesh,
        in_specs=(P("ctx", "head"), P(None, None, "head"), P("ctx", None), P("ctx", "head")),
        out_specs=(P("ctx", "head"), P("ctx", "head")),
        check_vma=False,
    )
```
